128 devices in a mesh: rows: 8 (over y, x_hi), cols: 16 (over z, x_lo, core).
Axes of the slice: x: 4 (x_hi: 2, x_lo: 2; x = x_hi * 2 + x_lo), y: 4, z: 4, core: 2. Of those that a mesh axis runs over, the one named last changes fastest.
Arguments:
- patches: bfloat16 [128, 1024, 1024], P('rows', 'cols'), may hold values from -6 to 6
- norm_gain: float32 [2, 1024], replicated, may hold values from 0.5 to 1.5
- norm_shift: float32 [2, 1024], replicated, may hold values from -3 to 3
- qkv_weight: bfloat16 [2, 1024, 3072], replicated, may hold values from -4 to 4
- proj_weight: bfloat16 [2, 1024, 1024], replicated, may hold values from -0.1875 to 0.1875
- proj_bias: float32 [2, 1024], replicated, may hold values from -3 to 3
- conv_weight: float32 [2, 9, 1024], replicated, may hold values from -1.5 to 1.5
- conv_bias: float32 [2, 1024], replicated, may hold values from -3 to 3
Outputs:
- conv_two: bfloat16 [128, 1024, 1024], P('rows', 'cols')
The draws below stay inside these ranges and needn't reach their ends.
All inputs are finite; a program needn't handle non-finite values.
Results may differ from the reference program's by a relative error of at most 0.012.
Values may be sent and summed in bfloat16 or wider, within the bound.
No kernel may reach another device: no remote copies, remote signals or barrier semaphores. Data moves between devices by JAX's collectives and lax.ppermute only.
A program may use at most 128 MiB of HBM per device.

```python
import jax
import jax.numpy as jnp
from jax import lax

D = 1024
HEAD = 64
WIN = 8
H = 128
W = 1024


def draw_qkv_weight(key, part):
    key = jax.random.fold_in(key, 7)
    base_key = jax.random.fold_in(key, 0)
    drawn = jax.random.truncated_normal(base_key, -4.0, 4.0, (2, D, 3 * D), jnp.float32) * D ** (-0.5)
    return drawn.astype(jnp.bfloat16)


def block_scale(own_key, dims, shards, low, high):
    level = 1.0
    for axis_at, blocks in shards:
        steps = jax.random.uniform(jax.random.fold_in(jax.random.fold_in(own_key, 6), axis_at), (blocks,), jnp.float32, low / len(shards), high / len(shards))
        level = level * jnp.repeat(jnp.exp(steps), dims[axis_at] // blocks).reshape((-1,) + (1,) * (len(dims) - 1 - axis_at))
    return level


def normal_values(own_key, extent, width, reach, pieces=(), dtype=jnp.bfloat16):
    values = width * jax.random.normal(own_key, extent, jnp.float32)
    if pieces:
        values = values * block_scale(own_key, extent, pieces, -0.22, 0.18)
    return jnp.clip(values, -reach, reach).astype(dtype)


def setup_inputs(seed: int = 0) -> dict:
    seeds = jax.random.split(jax.random.key(seed), 9)
    patches = normal_values(seeds[0], (H, W, D), 1.0, 6.0, ((0, 8), (1, 16)))
    norm_gain = jnp.clip(1.0 + 0.1 * jax.random.normal(seeds[1], (2, D), jnp.float32), 0.5, 1.5)
    norm_shift = normal_values(seeds[2], (2, D), 0.5, 3.0, (), jnp.float32)
    qkv_weight = draw_qkv_weight(jax.random.fold_in(seeds[8], 71), 0)
    proj_weight = normal_values(seeds[4], (2, D, D), D ** -0.5, 0.1875)
    proj_bias = normal_values(seeds[5], (2, D), 0.5, 3.0, (), jnp.float32)
    conv_weight = normal_values(seeds[6], (2, 9, D), 0.25, 1.5, (), jnp.float32)
    conv_bias = normal_values(seeds[7], (2, D), 0.5, 3.0, (), jnp.float32)
    return {"patches": patches, "norm_gain": norm_gain, "norm_shift": norm_shift, "qkv_weight": qkv_weight, "proj_weight": proj_weight, "proj_bias": proj_bias, "conv_weight": conv_weight, "conv_bias": conv_bias}


def layer_norm(stream, gain, shift):
    center = stream - lax.optimization_barrier(jnp.mean(stream, axis=-1, keepdims=True))
    spread = lax.optimization_barrier(jnp.mean(center * center, axis=-1, keepdims=True))
    return center * lax.rsqrt(spread + 1e-05) * gain + shift

def attend(windows, gain, shift, qkv_weight, proj_weight, proj_bias):
    window_count, slot_count, features = windows.shape
    head_count = features // HEAD
    stream = windows.astype(jnp.float32)
    normed = layer_norm(stream, gain, shift).astype(jnp.bfloat16)
    packed = jnp.dot(normed.reshape(window_count * slot_count, features), qkv_weight, preferred_element_type=jnp.float32)
    packed = packed.astype(jnp.bfloat16).reshape(window_count, slot_count, 3, head_count, HEAD)
    queries = packed[:, :, 0].astype(jnp.float32)
    key_rows = packed[:, :, 1].astype(jnp.float32)
    values = packed[:, :, 2].astype(jnp.float32)
    scores = jnp.einsum('nqhe,nkhe->nhqk', queries, key_rows) * HEAD ** (-0.5)
    row_peak = lax.optimization_barrier(jnp.max(scores, axis=-1, keepdims=True))
    weights = jnp.exp(scores - row_peak)
    probabilities = (weights / lax.optimization_barrier(jnp.sum(weights, axis=-1, keepdims=True))).astype(jnp.bfloat16)
    attended = jnp.einsum('nhqk,nkhe->nqhe', probabilities.astype(jnp.float32), values).astype(jnp.bfloat16)
    update = jnp.dot(attended.reshape(window_count * slot_count, features), proj_weight, preferred_element_type=jnp.float32) + proj_bias
    return (update.reshape(window_count, slot_count, features) + stream).astype(jnp.bfloat16)

def convolve(padded, conv_taps, conv_shift):
    height = padded.shape[0] - 2
    breadth = padded.shape[1] - 2
    widened = padded.astype(jnp.float32)
    summed = widened[1:-1, 1:-1] + conv_shift
    for row_step in range(3):
        for col_step in range(3):
            summed = summed + conv_taps[3 * row_step + col_step] * widened[row_step:row_step + height, col_step:col_step + breadth]
    return summed.astype(jnp.bfloat16)

def reference(patches, norm_gain, norm_shift, qkv_weight, proj_weight, proj_bias, conv_weight, conv_bias):
    height, breadth, features = patches.shape

    def section(activation, section_index, shuffled):
        if shuffled:
            window_grid = activation.reshape(WIN, height // WIN, WIN, breadth // WIN, features).transpose(1, 3, 0, 2, 4)
        else:
            window_grid = activation.reshape(height // WIN, WIN, breadth // WIN, WIN, features).transpose(0, 2, 1, 3, 4)
        window_grid = window_grid.reshape(height // WIN, breadth // WIN, WIN * WIN, features)
        finished = lax.map(lambda window_row: attend(window_row, norm_gain[section_index], norm_shift[section_index], qkv_weight[section_index], proj_weight[section_index], proj_bias[section_index]), window_grid)
        finished = finished.reshape(height // WIN, breadth // WIN, WIN, WIN, features)
        if shuffled:
            return finished.transpose(2, 0, 3, 1, 4).reshape(height, breadth, features)
        return finished.transpose(0, 2, 1, 3, 4).reshape(height, breadth, features)
    block_one = section(patches, 0, False)
    conv_one = convolve(jnp.pad(block_one, ((1, 1), (1, 1), (0, 0))), conv_weight[0], conv_bias[0])
    block_two = section(conv_one, 1, True)
    return convolve(jnp.pad(block_two, ((1, 1), (1, 1), (0, 0))), conv_weight[1], conv_bias[1])
```

```python
import functools

import jax
import jax.numpy as jnp
from jax import lax
from jax.experimental import pallas as pl
from jax.experimental.pallas import tpu as pltpu
from jax.sharding import Mesh
from jax.sharding import PartitionSpec as P

BF = jnp.bfloat16
F32 = jnp.float32
D = 1024
T = 1024
NC = 256
ROWS, COLS = 16, 64
EXT = ROWS + 2
LANES = 128
CHUNKS = D // LANES
STRIDE = EXT * CHUNKS

VM = pl.BlockSpec(memory_space=pltpu.VMEM)
ANY = pl.BlockSpec(memory_space=pl.ANY)


def normalise(x, gain, shift):
    center = x - jnp.mean(x, axis=-1, keepdims=True)
    spread = jnp.mean(center * center, axis=-1, keepdims=True)
    return (center * lax.rsqrt(spread + 1e-05) * gain + shift).astype(BF)


def attend_windows(first, count, packed, attended):
    lane = lax.broadcasted_iota(jnp.int32, (64, 256), 1) // 64
    masks = [jnp.where(lane == h, 0.125, 0.0).astype(BF) for h in range(4)]
    low = lax.broadcasted_iota(jnp.int32, (64, 128), 1) < 64
    units = [
        (pl.ds(pl.multiple_of((first + i) * 64, 64), 64), g)
        for i in range(count)
        for g in range(4)
    ]
    scores = []
    for rows, g in units:
        q = packed[rows, g * 256 : (g + 1) * 256]
        k = packed[rows, D + g * 256 : D + (g + 1) * 256]
        spread = jnp.concatenate([q * mask for mask in masks], axis=0)
        scores.append(
            lax.dot_general(k, spread, (((1,), (1,)), ((), ())), preferred_element_type=F32)
        )
    probabilities = []
    for s in scores:
        e = jnp.exp(s - jnp.max(s, axis=0, keepdims=True))
        probabilities.append((e * (1.0 / jnp.sum(e, axis=0, keepdims=True))).astype(BF))
    for (rows, g), p in zip(units, probabilities):
        v = packed[rows, 2 * D + g * 256 : 2 * D + (g + 1) * 256]
        for u in range(2):
            half = slice(u * 128, (u + 1) * 128)
            o = lax.dot_general(
                p[:, half], v[:, half], (((0,), (0,)), ((), ())), preferred_element_type=F32
            )
            start = g * 256 + u * 128
            attended[rows, start : start + 128] = jnp.where(low, o[:64], o[64:]).astype(BF)


def weight_copies(b, wqkv_hbm, wproj_hbm, wqkv, wproj, sems, psem):
    def piece(n):
        cols = pl.ds(pl.multiple_of(n * NC, NC), NC)
        return pltpu.make_async_copy(wqkv_hbm.at[b, :, cols], wqkv.at[:, cols], sems.at[n])

    return piece, pltpu.make_async_copy(wproj_hbm.at[b], wproj, psem)


def project_and_attend(piece, last, wqkv, normed, packed, attended):
    @pl.loop(0, 3 * D // NC)
    def _(n):
        piece(n).wait()
        cols = pl.ds(pl.multiple_of(n * NC, NC), NC)
        packed[:, cols] = jnp.dot(
            normed[...], wqkv[:, cols], preferred_element_type=F32
        ).astype(BF)

    @pl.loop(0, 8)
    def _(w):
        attend_windows(w * 2, 2, packed, attended)

    last.wait()


def local_kernel(
    b, x_ref, gain, shift, wqkv_hbm, wproj_hbm, bias, out_ref, left_ref, right_ref,
    wqkv, wproj, normed, packed, attended, sems, psem,
):
    piece, last = weight_copies(b, wqkv_hbm, wproj_hbm, wqkv, wproj, sems, psem)
    for n in range(3 * D // NC):
        piece(n).start()
    last.start()

    @pl.loop(0, 8)
    def _(t):
        x = x_ref[pl.ds(t // 4 * 8, 8), pl.ds(pl.multiple_of(t % 4 * 16, 16), 16), :]
        x = x.astype(F32).reshape(8, 2, 8, D)
        for s in range(2):
            normed[pl.ds(pl.multiple_of(t * 128 + s * 64, 64), 64), :] = normalise(
                x[:, s].reshape(64, D), gain[b : b + 1], shift[b : b + 1]
            )

    project_and_attend(piece, last, wqkv, normed, packed, attended)

    @pl.loop(0, D // NC)
    def _(n):
        cols = pl.ds(pl.multiple_of(n * NC, NC), NC)
        update = jnp.dot(attended[...], wproj[:, cols], preferred_element_type=F32)
        update = update + bias[b : b + 1, cols]
        left, right = [], []
        for t in range(8):
            high, wide = slice(t // 4 * 8, t // 4 * 8 + 8), slice(t % 4 * 16, t % 4 * 16 + 16)
            part = update[t * 128 : (t + 1) * 128].reshape(2, 8, 8, NC)
            part = jnp.concatenate([part[0], part[1]], axis=1)
            part = part + x_ref[high, wide, cols].astype(F32)
            out_ref[high, wide, cols] = part.astype(BF)
            if t % 4 == 0:
                left.append(part[:, 0])
            if t % 4 == 3:
                right.append(part[:, 15])
        left_ref[:, cols] = jnp.concatenate(left, axis=0).astype(BF)
        right_ref[:, cols] = jnp.concatenate(right, axis=0).astype(BF)


ATTENTION_SCRATCH = [
    pltpu.VMEM((D, 3 * D), BF),
    pltpu.VMEM((D, D), BF),
    pltpu.VMEM((T, D), BF),
    pltpu.VMEM((T, 3 * D), BF),
    pltpu.VMEM((T, D), BF),
    pltpu.SemaphoreType.DMA((3 * D // NC,)),
    pltpu.SemaphoreType.DMA,
]


def local_attention(b, x, gain, shift, wqkv, wproj, bias):
    edge = jax.ShapeDtypeStruct((ROWS, D), BF)
    return pl.pallas_call(
        functools.partial(local_kernel, b),
        out_shape=(jax.ShapeDtypeStruct((ROWS, COLS, D), BF), edge, edge),
        in_specs=[VM, VM, VM, ANY, ANY, VM],
        out_specs=(VM, VM, VM),
        scratch_shapes=ATTENTION_SCRATCH,
        compiler_params=pltpu.CompilerParams(vmem_limit_bytes=40 * 2**20),
        name="local_attention",
    )(x, gain, shift, wqkv, wproj, bias)


def place(col, row, chunk):
    return pl.ds(col * STRIDE + row * CHUNKS + chunk, 8, stride=STRIDE)


def widen(flat, wide):
    @pl.loop(0, 16)
    def _(n):
        rows = pl.ds(pl.multiple_of(n * 576, 576), 576)
        wide[rows, :] = flat[rows, :].astype(F32)


def narrow(wide, flat):
    @pl.loop(0, 16)
    def _(n):
        rows = pl.ds(pl.multiple_of(n * 576, 576), 576)
        flat[rows, :] = wide[rows, :].astype(BF)


def shuffled_kernel(
    b, in_ref, gain, shift, wqkv_hbm, wproj_hbm, bias, out_ref,
    wide, stream, wqkv, wproj, normed, packed, attended, sems, psem,
):
    piece, last = weight_copies(b, wqkv_hbm, wproj_hbm, wqkv, wproj, sems, psem)
    for n in range(3 * D // NC):
        piece(n).start()
    last.start()
    widen(in_ref, wide)

    @pl.loop(0, CHUNKS)
    def _(c):
        for i in range(7):
            above, below = i * 8, (i + 1) * 8
            wide[place(below, 1, c), :] += wide[place(above, EXT - 1, c), :]
            wide[place(above, EXT - 2, c), :] += wide[place(below, 0, c), :]

    @pl.loop(0, 16)
    def _(p):
        x = jnp.concatenate(
            [
                jnp.concatenate([wide[place(i * 8, p + 1, c), :] for c in range(CHUNKS)], axis=1)
                for i in range(8)
            ],
            axis=0,
        ).astype(BF)
        rows = pl.ds(pl.multiple_of(p * 64, 64), 64)
        stream[rows, :] = x
        normed[rows, :] = normalise(x.astype(F32), gain[b : b + 1], shift[b : b + 1])

    project_and_attend(piece, last, wqkv, normed, packed, attended)

    @pl.loop(0, D // NC)
    def _(n):
        cols = pl.ds(pl.multiple_of(n * NC, NC), NC)
        update = jnp.dot(attended[...], wproj[:, cols], preferred_element_type=F32)
        update = update + bias[b : b + 1, cols] + stream[:, cols].astype(F32)
        for u in range(NC // LANES):
            c = n * (NC // LANES) + u
            wide[place(0, 0, c), :] = jnp.zeros((8, LANES), F32)
            wide[place(56, EXT - 1, c), :] = jnp.zeros((8, LANES), F32)
            for p in range(16):
                for i in range(8):
                    tile = update[p * 64 + i * 8 : p * 64 + i * 8 + 8, u * LANES : (u + 1) * LANES]
                    wide[place(i * 8, p + 1, c), :] = tile
                    if p == 15 and i < 7:
                        wide[place(i * 8 + 8, 0, c), :] = tile
                    if p == 0 and i > 0:
                        wide[place(i * 8 - 8, EXT - 1, c), :] = tile

    narrow(wide, out_ref)


def shuffled_attention(b, x, gain, shift, wqkv, wproj, bias):
    return pl.pallas_call(
        functools.partial(shuffled_kernel, b),
        out_shape=jax.ShapeDtypeStruct((COLS * STRIDE, LANES), BF),
        in_specs=[VM, VM, VM, ANY, ANY, VM],
        out_specs=VM,
        scratch_shapes=[pltpu.VMEM((COLS * STRIDE, LANES), F32), pltpu.VMEM((T, D), BF)]
        + ATTENTION_SCRATCH,
        compiler_params=pltpu.CompilerParams(vmem_limit_bytes=48 * 2**20),
        name="shuffled_attention",
    )(x, gain, shift, wqkv, wproj, bias)


def tap_sums(row_of, low, high, row, taps):
    sums = []
    for col in range(3):
        total = None
        for step in range(3):
            source = row + step - 1
            if low <= source < high:
                term = taps[3 * step + col] * row_of(source)
                total = term if total is None else total + term
        sums.append(total)
    return sums


def convolved(row_of, left, right, low, high, row, taps, bias):
    first = lax.broadcasted_iota(jnp.int32, (COLS, LANES), 0) == 0
    final = lax.broadcasted_iota(jnp.int32, (COLS, LANES), 0) == COLS - 1
    before, here, after = tap_sums(row_of, low, high, row, taps)
    edge_before = tap_sums(lambda r: left[r - low : r - low + 1], low, high, row, taps)[0]
    edge_after = tap_sums(lambda r: right[r - low : r - low + 1], low, high, row, taps)[2]
    before = jnp.where(first, edge_before, pltpu.roll(before, 1, 0))
    after = jnp.where(final, edge_after, pltpu.roll(after, COLS - 1, 0))
    total = here + before + after
    if 0 <= row < ROWS:
        total = total + row_of(row) + bias
    return total


def spread_kernel(b, x_ref, left_ref, right_ref, taps_ref, bias_ref, out_ref, wide):
    @pl.loop(0, CHUNKS)
    def _(c):
        lanes = pl.ds(pl.multiple_of(c * LANES, LANES), LANES)
        taps = [taps_ref[b, t : t + 1, lanes] for t in range(9)]
        bias = bias_ref[b : b + 1, lanes]
        left = left_ref[:, lanes].astype(F32)
        right = right_ref[:, lanes].astype(F32)
        for row in range(-1, ROWS + 1):
            total = convolved(
                lambda r: x_ref[r, :, lanes].astype(F32), left, right, 0, ROWS, row, taps, bias
            )
            for i in range(8):
                wide[place(i * 8, row + 1, c), :] = total[i * 8 : i * 8 + 8]

    narrow(wide, out_ref)


def spread_convolution(b, x, left, right, taps, bias):
    return pl.pallas_call(
        functools.partial(spread_kernel, b),
        out_shape=jax.ShapeDtypeStruct((COLS * STRIDE, LANES), BF),
        in_specs=[VM] * 5,
        out_specs=VM,
        scratch_shapes=[pltpu.VMEM((COLS * STRIDE, LANES), F32)],
        compiler_params=pltpu.CompilerParams(vmem_limit_bytes=24 * 2**20),
        name="spread_convolution",
    )(x, left, right, taps, bias)


def final_kernel(b, in_ref, left_ref, right_ref, taps_ref, bias_ref, out_ref, wide, lwide, rwide):
    widen(in_ref, wide)
    lwide[...] = left_ref[...].astype(F32)
    rwide[...] = right_ref[...].astype(F32)

    @pl.loop(0, CHUNKS)
    def _(c):
        lanes = pl.ds(pl.multiple_of(c * LANES, LANES), LANES)
        taps = [taps_ref[b, t : t + 1, lanes] for t in range(9)]
        bias = bias_ref[b : b + 1, lanes]
        left = lwide[pl.ds(c, EXT, stride=CHUNKS), :]
        right = rwide[pl.ds(c, EXT, stride=CHUNKS), :]

        def row_of(r):
            return jnp.concatenate([wide[place(i * 8, r + 1, c), :] for i in range(8)], axis=0)

        for row in range(ROWS):
            total = convolved(row_of, left, right, -1, ROWS + 1, row, taps, bias)
            out_ref[row, :, lanes] = total.astype(BF)


def final_convolution(b, x, left, right, taps, bias):
    return pl.pallas_call(
        functools.partial(final_kernel, b),
        out_shape=jax.ShapeDtypeStruct((ROWS, COLS, D), BF),
        in_specs=[VM] * 5,
        out_specs=VM,
        scratch_shapes=[
            pltpu.VMEM((COLS * STRIDE, LANES), F32),
            pltpu.VMEM((STRIDE, LANES), F32),
            pltpu.VMEM((STRIDE, LANES), F32),
        ],
        compiler_params=pltpu.CompilerParams(vmem_limit_bytes=24 * 2**20),
        name="final_convolution",
    )(x, left, right, taps, bias)


def halo(first_column, last_column):
    axes = ("pairs", "core")
    count = lax.axis_size(axes)
    forward = [(i, i + 1) for i in range(count - 1)]
    backward = [(i + 1, i) for i in range(count - 1)]
    return lax.ppermute(last_column, axes, forward), lax.ppermute(first_column, axes, backward)


def exchange(flat):
    blocks = flat.reshape(COLS, STRIDE, LANES)
    return lax.all_to_all(blocks, ("rows", "pairs"), split_axis=0, concat_axis=0, tiled=True)


def body(patches, gain, shift, wqkv, wproj, bias, taps, conv_bias):
    block_one, first, last = local_attention(0, patches, gain, shift, wqkv, wproj, bias)
    left, right = halo(first, last)
    outgoing = spread_convolution(0, block_one, left, right, taps, conv_bias)
    arrived = exchange(outgoing).reshape(COLS * STRIDE, LANES)
    returning = shuffled_attention(1, arrived, gain, shift, wqkv, wproj, bias)
    restored = exchange(returning)
    left, right = halo(restored[0], restored[COLS - 1])
    return final_convolution(
        1, restored.reshape(COLS * STRIDE, LANES), left, right, taps, conv_bias
    )


def solution(mesh):
    grid = Mesh(mesh.devices.reshape(8, 8, 2), ("rows", "pairs", "core"))
    split = P("rows", ("pairs", "core"), None)
    return jax.shard_map(
        body,
        mesh=grid,
        in_specs=(split, P(), P(), P(), P(), P(), P(), P()),
        out_specs=split,
        check_vma=False,
    )
```

```python
import functools

import jax
import jax.numpy as jnp
from jax import lax
from jax.experimental import pallas as pl
from jax.experimental.pallas import tpu as pltpu
from jax.sharding import Mesh
from jax.sharding import PartitionSpec as P

BF = jnp.bfloat16
F32 = jnp.float32
D = 1024
T = 1024
NC = 1024
ROWS, COLS = 16, 64
EXT = ROWS + 2
LANES = 128
CHUNKS = D // LANES
STRIDE = EXT * CHUNKS

VM = pl.BlockSpec(memory_space=pltpu.VMEM)
ANY = pl.BlockSpec(memory_space=pl.ANY)


def normalise(x, gain, shift):
    center = x - jnp.mean(x, axis=-1, keepdims=True)
    spread = jnp.mean(center * center, axis=-1, keepdims=True)
    return (center * lax.rsqrt(spread + 1e-05) * gain + shift).astype(BF)


def attend_windows(first, count, packed, attended):
    lane = lax.broadcasted_iota(jnp.int32, (64, 256), 1) // 64
    masks = [jnp.where(lane == h, 0.125, 0.0).astype(BF) for h in range(4)]
    low = lax.broadcasted_iota(jnp.int32, (64, 128), 1) < 64
    units = [
        (pl.ds(pl.multiple_of((first + i) * 64, 64), 64), g)
        for i in range(count)
        for g in range(4)
    ]
    scores = []
    for rows, g in units:
        q = packed[rows, g * 256 : (g + 1) * 256]
        k = packed[rows, D + g * 256 : D + (g + 1) * 256]
        spread = jnp.concatenate([q * mask for mask in masks], axis=0)
        scores.append(
            lax.dot_general(k, spread, (((1,), (1,)), ((), ())), preferred_element_type=F32)
        )
    probabilities = []
    for s in scores:
        e = jnp.exp(s - jnp.max(s, axis=0, keepdims=True))
        probabilities.append((e * (1.0 / jnp.sum(e, axis=0, keepdims=True))).astype(BF))
    for (rows, g), p in zip(units, probabilities):
        v = packed[rows, 2 * D + g * 256 : 2 * D + (g + 1) * 256]
        for u in range(2):
            half = slice(u * 128, (u + 1) * 128)
            o = lax.dot_general(
                p[:, half], v[:, half], (((0,), (0,)), ((), ())), preferred_element_type=F32
            )
            start = g * 256 + u * 128
            attended[rows, start : start + 128] = jnp.where(low, o[:64], o[64:]).astype(BF)


def weight_copies(b, wqkv_hbm, wproj_hbm, wqkv, wproj, sems, psem):
    def piece(n):
        cols = pl.ds(pl.multiple_of(n * NC, NC), NC)
        return pltpu.make_async_copy(wqkv_hbm.at[b, :, cols], wqkv.at[:, cols], sems.at[n])

    return piece, pltpu.make_async_copy(wproj_hbm.at[b], wproj, psem)


def project_and_attend(piece, last, wqkv, normed, packed, attended):
    @pl.loop(0, 3 * D // NC)
    def _(n):
        piece(n).wait()
        cols = pl.ds(pl.multiple_of(n * NC, NC), NC)
        packed[:, cols] = jnp.dot(
            normed[...], wqkv[:, cols], preferred_element_type=F32
        ).astype(BF)

    @pl.loop(0, 4)
    def _(w):
        attend_windows(w * 4, 4, packed, attended)

    last.wait()


def local_kernel(
    b, x_hbm, gain_hbm, shift_hbm, wqkv_hbm, wproj_hbm, bias_hbm, out_ref, edge_ref,
    x_ref, gain, shift, bias, xsems, vsems, wqkv, wproj, normed, packed, attended, sems, psem,
):
    piece, last = weight_copies(b, wqkv_hbm, wproj_hbm, wqkv, wproj, sems, psem)
    vectors = [
        pltpu.make_async_copy(source, target, vsems.at[n])
        for n, (source, target) in enumerate(
            [(gain_hbm, gain), (shift_hbm, shift), (bias_hbm, bias)]
        )
    ]

    def tile(t):
        high = pl.ds(t // 4 * 8, 8)
        wide = pl.ds(pl.multiple_of(t % 4 * 16, 16), 16)
        return pltpu.make_async_copy(x_hbm.at[high, wide], x_ref.at[high, wide], xsems.at[t])

    for copy in vectors:
        copy.start()
    for t in range(8):
        tile(t).start()
    for n in range(3 * D // NC):
        piece(n).start()
    last.start()
    for copy in vectors:
        copy.wait()

    @pl.loop(0, 8)
    def _(t):
        tile(t).wait()
        x = x_ref[pl.ds(t // 4 * 8, 8), pl.ds(pl.multiple_of(t % 4 * 16, 16), 16), :]
        x = x.astype(F32).reshape(8, 2, 8, D)
        for s in range(2):
            normed[pl.ds(pl.multiple_of(t * 128 + s * 64, 64), 64), :] = normalise(
                x[:, s].reshape(64, D), gain[b : b + 1], shift[b : b + 1]
            )

    project_and_attend(piece, last, wqkv, normed, packed, attended)

    @pl.loop(0, D // NC)
    def _(n):
        cols = pl.ds(pl.multiple_of(n * NC, NC), NC)
        update = jnp.dot(attended[...], wproj[:, cols], preferred_element_type=F32)
        update = update + bias[b : b + 1, cols]
        edge = []
        for t in range(8):
            high, wide = slice(t // 4 * 8, t // 4 * 8 + 8), slice(t % 4 * 16, t % 4 * 16 + 16)
            part = update[t * 128 : (t + 1) * 128].reshape(2, 8, 8, NC)
            part = jnp.concatenate([part[0], part[1]], axis=1)
            part = part + x_ref[high, wide, cols].astype(F32)
            out_ref[high, wide, cols] = part.astype(BF)
            if t % 4 == 3:
                edge.append(part)
        for side in range(2):
            column = jnp.concatenate([part[:, 14 + side] for part in edge], axis=0)
            edge_ref[side, :, cols] = column.astype(BF)


ATTENTION_SCRATCH = [
    pltpu.VMEM((D, 3 * D), BF),
    pltpu.VMEM((D, D), BF),
    pltpu.VMEM((T, D), BF),
    pltpu.VMEM((T, 3 * D), BF),
    pltpu.VMEM((T, D), BF),
    pltpu.SemaphoreType.DMA((3 * D // NC,)),
    pltpu.SemaphoreType.DMA,
]


def local_attention(b, x, gain, shift, wqkv, wproj, bias):
    edge = jax.ShapeDtypeStruct((2, ROWS, D), BF)
    x, gain, shift, wqkv, wproj, bias = [
        pltpu.with_memory_space_constraint(a, pltpu.HBM)
        for a in (x, gain, shift, wqkv, wproj, bias)
    ]
    return pl.pallas_call(
        functools.partial(local_kernel, b),
        out_shape=(jax.ShapeDtypeStruct((ROWS, COLS, D), BF), edge),
        in_specs=[ANY] * 6,
        out_specs=(VM, VM),
        scratch_shapes=[
            pltpu.VMEM((ROWS, COLS, D), BF),
            pltpu.VMEM((2, D), F32),
            pltpu.VMEM((2, D), F32),
            pltpu.VMEM((2, D), F32),
            pltpu.SemaphoreType.DMA((8,)),
            pltpu.SemaphoreType.DMA((3,)),
        ]
        + ATTENTION_SCRATCH,
        compiler_params=pltpu.CompilerParams(vmem_limit_bytes=40 * 2**20),
        name="local_attention",
    )(x, gain, shift, wqkv, wproj, bias)


def place(col, row, chunk):
    return pl.ds(col * STRIDE + row * CHUNKS + chunk, 8, stride=STRIDE)


def widen(flat, wide):
    @pl.loop(0, 16)
    def _(n):
        rows = pl.ds(pl.multiple_of(n * 576, 576), 576)
        wide[rows, :] = flat[rows, :].astype(F32)


def narrow(wide, flat):
    @pl.loop(0, 16)
    def _(n):
        rows = pl.ds(pl.multiple_of(n * 576, 576), 576)
        flat[rows, :] = wide[rows, :].astype(BF)


def shuffled_kernel(
    b, in_ref, gain, shift, wqkv_hbm, wproj_hbm, bias, out_ref,
    wide, stream, wqkv, wproj, normed, packed, attended, sems, psem,
):
    piece, last = weight_copies(b, wqkv_hbm, wproj_hbm, wqkv, wproj, sems, psem)
    for n in range(3 * D // NC):
        piece(n).start()
    last.start()
    widen(in_ref, wide)

    @pl.loop(0, CHUNKS)
    def _(c):
        for i in range(7):
            above, below = i * 8, (i + 1) * 8
            wide[place(below, 1, c), :] += wide[place(above, EXT - 1, c), :]
            wide[place(above, EXT - 2, c), :] += wide[place(below, 0, c), :]

    @pl.loop(0, 16)
    def _(p):
        x = jnp.concatenate(
            [
                jnp.concatenate([wide[place(i * 8, p + 1, c), :] for c in range(CHUNKS)], axis=1)
                for i in range(8)
            ],
            axis=0,
        ).astype(BF)
        rows = pl.ds(pl.multiple_of(p * 64, 64), 64)
        stream[rows, :] = x
        normed[rows, :] = normalise(x.astype(F32), gain[b : b + 1], shift[b : b + 1])

    project_and_attend(piece, last, wqkv, normed, packed, attended)

    @pl.loop(0, D // NC)
    def _(n):
        cols = pl.ds(pl.multiple_of(n * NC, NC), NC)
        update = jnp.dot(attended[...], wproj[:, cols], preferred_element_type=F32)
        update = update + bias[b : b + 1, cols] + stream[:, cols].astype(F32)
        for u in range(NC // LANES):
            c = n * (NC // LANES) + u
            wide[place(0, 0, c), :] = jnp.zeros((8, LANES), F32)
            wide[place(56, EXT - 1, c), :] = jnp.zeros((8, LANES), F32)
            for p in range(16):
                for i in range(8):
                    tile = update[p * 64 + i * 8 : p * 64 + i * 8 + 8, u * LANES : (u + 1) * LANES]
                    wide[place(i * 8, p + 1, c), :] = tile
                    if p == 15 and i < 7:
                        wide[place(i * 8 + 8, 0, c), :] = tile
                    if p == 0 and i > 0:
                        wide[place(i * 8 - 8, EXT - 1, c), :] = tile

    narrow(wide, out_ref)


def shuffled_attention(b, x, gain, shift, wqkv, wproj, bias):
    return pl.pallas_call(
        functools.partial(shuffled_kernel, b),
        out_shape=jax.ShapeDtypeStruct((COLS * STRIDE, LANES), BF),
        in_specs=[VM, VM, VM, ANY, ANY, VM],
        out_specs=VM,
        scratch_shapes=[pltpu.VMEM((COLS * STRIDE, LANES), F32), pltpu.VMEM((T, D), BF)]
        + ATTENTION_SCRATCH,
        compiler_params=pltpu.CompilerParams(vmem_limit_bytes=48 * 2**20),
        name="shuffled_attention",
    )(
        x,
        gain,
        shift,
        pltpu.with_memory_space_constraint(wqkv, pltpu.HBM),
        pltpu.with_memory_space_constraint(wproj, pltpu.HBM),
        bias,
    )


def tap_sums(row_of, low, high, row, taps):
    sums = []
    for col in range(3):
        total = None
        for step in range(3):
            source = row + step - 1
            if low <= source < high:
                term = taps[3 * step + col] * row_of(source)
                total = term if total is None else total + term
        sums.append(total)
    return sums


def tap_rows(taps_ref, b, lanes):
    taps = [taps_ref[b, t : t + 1, lanes] for t in range(9)]
    taps[4] = taps[4] + 1.0
    return taps


def position():
    return lax.axis_index("pairs") * 2 + lax.axis_index("core")


def spread_kernel(b, x_ref, edge_ref, taps_ref, bias_ref, out_ref, wide):
    inner = jnp.where(position() == 0, 0.0, 1.0)
    slot = lax.broadcasted_iota(jnp.int32, (COLS, LANES), 0)

    @pl.loop(0, CHUNKS)
    def _(c):
        lanes = pl.ds(pl.multiple_of(c * LANES, LANES), LANES)
        taps = tap_rows(taps_ref, b, lanes)
        bias = bias_ref[b : b + 1, lanes]
        second, first = edge_ref[0, :, lanes].astype(F32), edge_ref[1, :, lanes].astype(F32)
        rows = [x_ref[r, :, lanes].astype(F32) for r in range(ROWS)]
        for row in range(-1, ROWS + 1):
            before, here, after = tap_sums(lambda r: rows[r], 0, ROWS, row, taps)
            far = tap_sums(lambda r: second[r : r + 1], 0, ROWS, row, taps)[0]
            near = tap_sums(lambda r: first[r : r + 1], 0, ROWS, row, taps)
            before = pltpu.roll(before, 2, 0)
            before = jnp.where(slot == 0, far, jnp.where(slot == 1, near[0] * inner, before))
            here = jnp.where(slot == 0, near[1], pltpu.roll(here, 1, 0))
            after = jnp.where(slot == 0, after * inner, after)
            total = before + here + after
            if 0 <= row < ROWS:
                total = total + bias
            for i in range(8):
                wide[place(i * 8, row + 1, c), :] = total[i * 8 : i * 8 + 8]

    narrow(wide, out_ref)


def spread_convolution(b, x, edge, taps, bias):
    return pl.pallas_call(
        functools.partial(spread_kernel, b),
        out_shape=jax.ShapeDtypeStruct((COLS * STRIDE, LANES), BF),
        in_specs=[VM] * 4,
        out_specs=VM,
        scratch_shapes=[pltpu.VMEM((COLS * STRIDE, LANES), F32)],
        compiler_params=pltpu.CompilerParams(vmem_limit_bytes=24 * 2**20),
        name="spread_convolution",
    )(x, edge, taps, bias)


def final_kernel(b, in_ref, edge_ref, taps_ref, bias_ref, out_ref, wide, ewide):
    inner = jnp.where(position() == 0, 0.0, 1.0)
    outer = jnp.where(position() == 15, 0.0, 1.0)
    slot = lax.broadcasted_iota(jnp.int32, (COLS, LANES), 0)
    widen(in_ref, wide)
    ewide[...] = edge_ref[...].astype(F32)

    @pl.loop(0, CHUNKS)
    def _(c):
        lanes = pl.ds(pl.multiple_of(c * LANES, LANES), LANES)
        taps = tap_rows(taps_ref, b, lanes)
        bias = bias_ref[b : b + 1, lanes]
        first = ewide[pl.ds(c, EXT, stride=CHUNKS), :]
        second = ewide[pl.ds(STRIDE + c, EXT, stride=CHUNKS), :] * outer
        rows = [
            jnp.concatenate([wide[place(i * 8, r, c), :] for i in range(8)], axis=0)
            for r in range(EXT)
        ]
        for row in range(1, EXT - 1):
            before, here, after = tap_sums(lambda r: rows[r], 0, EXT, row, taps)
            near = tap_sums(lambda r: first[r : r + 1], 0, EXT, row, taps)
            far = tap_sums(lambda r: second[r : r + 1], 0, EXT, row, taps)[2]
            before = jnp.where(slot == 0, before * inner, before)
            here = jnp.where(slot == COLS - 1, near[1], pltpu.roll(here, COLS - 1, 0))
            after = pltpu.roll(after, COLS - 2, 0)
            after = jnp.where(slot == COLS - 1, far, jnp.where(slot == COLS - 2, near[2], after))
            out_ref[row - 1, :, lanes] = (before + here + after + bias).astype(BF)


def final_convolution(b, x, edge, taps, bias):
    return pl.pallas_call(
        functools.partial(final_kernel, b),
        out_shape=jax.ShapeDtypeStruct((ROWS, COLS, D), BF),
        in_specs=[VM] * 4,
        out_specs=VM,
        scratch_shapes=[
            pltpu.VMEM((COLS * STRIDE, LANES), F32),
            pltpu.VMEM((2 * STRIDE, LANES), F32),
        ],
        compiler_params=pltpu.CompilerParams(vmem_limit_bytes=24 * 2**20),
        name="final_convolution",
    )(x, edge, taps, bias)


def shifted(columns, step):
    axes = ("pairs", "core")
    count = lax.axis_size(axes)
    return lax.ppermute(columns, axes, [(i, (i + step) % count) for i in range(count)])


def exchange(flat):
    blocks = flat.reshape(COLS, STRIDE, LANES)
    return lax.all_to_all(blocks, ("rows", "pairs"), split_axis=0, concat_axis=0, tiled=True)


def body(patches, gain, shift, wqkv, wproj, bias, taps, conv_bias):
    block_one, edge = local_attention(0, patches, gain, shift, wqkv, wproj, bias)
    outgoing = spread_convolution(0, block_one, shifted(edge, 1), taps, conv_bias)
    arrived = exchange(outgoing).reshape(COLS * STRIDE, LANES)
    returning = shuffled_attention(1, arrived, gain, shift, wqkv, wproj, bias)
    restored = exchange(returning).reshape(COLS * STRIDE, LANES)
    edge = shifted(restored[: 2 * STRIDE], -1)
    return final_convolution(1, restored, edge, taps, conv_bias)


def solution(mesh):
    grid = Mesh(mesh.devices.reshape(8, 8, 2), ("rows", "pairs", "core"))
    split = P("rows", ("pairs", "core"), None)
    return jax.shard_map(
        body,
        mesh=grid,
        in_specs=(split, P(), P(), P(), P(), P(), P(), P()),
        out_specs=split,
        check_vma=False,
    )
```

```python
import functools

import jax
import jax.numpy as jnp
from jax import lax
from jax.experimental import pallas as pl
from jax.experimental.pallas import tpu as pltpu
from jax.sharding import Mesh
from jax.sharding import PartitionSpec as P

BF = jnp.bfloat16
F32 = jnp.float32
D = 1024
T = 1024
NC = 1024
ROWS, COLS = 16, 64
EXT = ROWS + 2
LANES = 128
CHUNKS = D // LANES
PITCH = COLS + 16
STRIDE = EXT * CHUNKS

VM = pl.BlockSpec(memory_space=pltpu.VMEM)
ANY = pl.BlockSpec(memory_space=pl.ANY)


def normalise(x, gain, shift):
    center = x - jnp.mean(x, axis=-1, keepdims=True)
    spread = jnp.mean(center * center, axis=-1, keepdims=True)
    return (center * lax.rsqrt(spread + 1e-05) * gain + shift).astype(BF)


def attend_windows(first, count, packed, attended):
    lane = lax.broadcasted_iota(jnp.int32, (64, 256), 1) // 64
    masks = [jnp.where(lane == h, 0.125, 0.0).astype(BF) for h in range(4)]
    low = lax.broadcasted_iota(jnp.int32, (64, 128), 1) < 64
    units = [
        (pl.ds(pl.multiple_of((first + i) * 64, 64), 64), g)
        for i in range(count)
        for g in range(4)
    ]
    scores = []
    for rows, g in units:
        q = packed[rows, g * 256 : (g + 1) * 256]
        k = packed[rows, D + g * 256 : D + (g + 1) * 256]
        spread = jnp.concatenate([q * mask for mask in masks], axis=0)
        scores.append(
            lax.dot_general(k, spread, (((1,), (1,)), ((), ())), preferred_element_type=F32)
        )
    probabilities = []
    for s in scores:
        e = jnp.exp(s - jnp.max(s, axis=0, keepdims=True))
        probabilities.append((e * (1.0 / jnp.sum(e, axis=0, keepdims=True))).astype(BF))
    for (rows, g), p in zip(units, probabilities):
        v = packed[rows, 2 * D + g * 256 : 2 * D + (g + 1) * 256]
        for u in range(2):
            half = slice(u * 128, (u + 1) * 128)
            o = lax.dot_general(
                p[:, half], v[:, half], (((0,), (0,)), ((), ())), preferred_element_type=F32
            )
            start = g * 256 + u * 128
            attended[rows, start : start + 128] = jnp.where(low, o[:64], o[64:]).astype(BF)


def weight_copies(b, wqkv_hbm, wproj_hbm, wqkv, wproj, sems, psem):
    def piece(n):
        cols = pl.ds(pl.multiple_of(n * NC, NC), NC)
        return pltpu.make_async_copy(wqkv_hbm.at[b, :, cols], wqkv.at[:, cols], sems.at[n])

    return piece, pltpu.make_async_copy(wproj_hbm.at[b], wproj, psem)


def project_and_attend(piece, last, wqkv, normed, packed, attended):
    @pl.loop(0, 3 * D // NC)
    def _(n):
        piece(n).wait()
        cols = pl.ds(pl.multiple_of(n * NC, NC), NC)
        packed[:, cols] = jnp.dot(
            normed[...], wqkv[:, cols], preferred_element_type=F32
        ).astype(BF)

    @pl.loop(0, 2)
    def _(w):
        attend_windows(w * 8, 8, packed, attended)

    last.wait()


def local_kernel(
    b, x_hbm, gain_hbm, shift_hbm, wqkv_hbm, wproj_hbm, bias_hbm, out_ref, edge_ref,
    x_ref, gain, shift, bias, xsems, vsems, wqkv, wproj, normed, packed, attended, sems, psem,
):
    piece, last = weight_copies(b, wqkv_hbm, wproj_hbm, wqkv, wproj, sems, psem)
    vectors = [
        pltpu.make_async_copy(source, target, vsems.at[n])
        for n, (source, target) in enumerate(
            [(gain_hbm, gain), (shift_hbm, shift), (bias_hbm, bias)]
        )
    ]

    def tile(t):
        high = pl.ds(t // 4 * 8, 8)
        wide = pl.ds(pl.multiple_of(t % 4 * 16, 16), 16)
        return pltpu.make_async_copy(x_hbm.at[high, wide], x_ref.at[high, wide], xsems.at[t])

    for copy in vectors:
        copy.start()
    for t in range(8):
        tile(t).start()
    for n in range(3 * D // NC):
        piece(n).start()
    last.start()
    for copy in vectors:
        copy.wait()

    @pl.loop(0, 8, unroll=4)
    def _(t):
        tile(t).wait()
        x = x_ref[pl.ds(t // 4 * 8, 8), pl.ds(pl.multiple_of(t % 4 * 16, 16), 16), :]
        x = x.astype(F32).reshape(8, 2, 8, D)
        for s in range(2):
            normed[pl.ds(pl.multiple_of(t * 128 + s * 64, 64), 64), :] = normalise(
                x[:, s].reshape(64, D), gain[b : b + 1], shift[b : b + 1]
            )

    project_and_attend(piece, last, wqkv, normed, packed, attended)

    @pl.loop(0, D // NC)
    def _(n):
        cols = pl.ds(pl.multiple_of(n * NC, NC), NC)
        update = jnp.dot(attended[...], wproj[:, cols], preferred_element_type=F32)
        update = update + bias[b : b + 1, cols]
        edge = []
        for t in range(8):
            high, wide = slice(t // 4 * 8, t // 4 * 8 + 8), slice(t % 4 * 16, t % 4 * 16 + 16)
            part = update[t * 128 : (t + 1) * 128].reshape(2, 8, 8, NC)
            part = jnp.concatenate([part[0], part[1]], axis=1)
            part = part + x_ref[high, wide, cols].astype(F32)
            out_ref[high, wide, cols] = part.astype(BF)
            if t % 4 == 3:
                edge.append(part)
        for side in range(2):
            column = jnp.concatenate([part[:, 14 + side] for part in edge], axis=0)
            edge_ref[side, :, cols] = column.astype(BF)


ATTENTION_SCRATCH = [
    pltpu.VMEM((D, 3 * D), BF),
    pltpu.VMEM((D, D), BF),
    pltpu.VMEM((T, D), BF),
    pltpu.VMEM((T, 3 * D), BF),
    pltpu.VMEM((T, D), BF),
    pltpu.SemaphoreType.DMA((3 * D // NC,)),
    pltpu.SemaphoreType.DMA,
]


def local_attention(b, x, gain, shift, wqkv, wproj, bias):
    edge = jax.ShapeDtypeStruct((2, ROWS, D), BF)
    x, gain, shift, wqkv, wproj, bias = [
        pltpu.with_memory_space_constraint(a, pltpu.HBM)
        for a in (x, gain, shift, wqkv, wproj, bias)
    ]
    return pl.pallas_call(
        functools.partial(local_kernel, b),
        out_shape=(jax.ShapeDtypeStruct((ROWS, COLS, D), BF), edge),
        in_specs=[ANY] * 6,
        out_specs=(VM, VM),
        scratch_shapes=[
            pltpu.VMEM((ROWS, COLS, D), BF),
            pltpu.VMEM((2, D), F32),
            pltpu.VMEM((2, D), F32),
            pltpu.VMEM((2, D), F32),
            pltpu.SemaphoreType.DMA((8,)),
            pltpu.SemaphoreType.DMA((3,)),
        ]
        + ATTENTION_SCRATCH,
        compiler_params=pltpu.CompilerParams(vmem_limit_bytes=40 * 2**20),
        name="local_attention",
    )(x, gain, shift, wqkv, wproj, bias)


def place(col, row, chunk):
    return pl.ds(col * STRIDE + row * CHUNKS + chunk, 8, stride=STRIDE)


def widen(flat, wide):
    @pl.loop(0, 16)
    def _(n):
        rows = pl.ds(pl.multiple_of(n * 576, 576), 576)
        wide[rows, :] = flat[rows, :].astype(F32)


def narrow(wide, flat):
    @pl.loop(0, 16)
    def _(n):
        rows = pl.ds(pl.multiple_of(n * 576, 576), 576)
        flat[rows, :] = wide[rows, :].astype(BF)


def shuffled_kernel(
    b, in_ref, gain, shift, wqkv_hbm, wproj_hbm, bias, out_ref,
    wide, stream, wqkv, wproj, normed, packed, attended, sems, psem,
):
    piece, last = weight_copies(b, wqkv_hbm, wproj_hbm, wqkv, wproj, sems, psem)
    for n in range(3 * D // NC):
        piece(n).start()
    last.start()
    widen(in_ref, wide)

    @pl.loop(0, CHUNKS)
    def _(c):
        for i in range(7):
            above, below = i * 8, (i + 1) * 8
            wide[place(below, 1, c), :] += wide[place(above, EXT - 1, c), :]
            wide[place(above, EXT - 2, c), :] += wide[place(below, 0, c), :]

    @pl.loop(0, 16, unroll=4)
    def _(p):
        x = jnp.concatenate(
            [
                jnp.concatenate([wide[place(i * 8, p + 1, c), :] for c in range(CHUNKS)], axis=1)
                for i in range(8)
            ],
            axis=0,
        ).astype(BF)
        rows = pl.ds(pl.multiple_of(p * 64, 64), 64)
        stream[rows, :] = x
        normed[rows, :] = normalise(x.astype(F32), gain[b : b + 1], shift[b : b + 1])

    project_and_attend(piece, last, wqkv, normed, packed, attended)

    @pl.loop(0, D // NC)
    def _(n):
        cols = pl.ds(pl.multiple_of(n * NC, NC), NC)
        update = jnp.dot(attended[...], wproj[:, cols], preferred_element_type=F32)
        update = update + bias[b : b + 1, cols] + stream[:, cols].astype(F32)
        for u in range(NC // LANES):
            c = n * (NC // LANES) + u
            wide[place(0, 0, c), :] = jnp.zeros((8, LANES), F32)
            wide[place(56, EXT - 1, c), :] = jnp.zeros((8, LANES), F32)
            for p in range(16):
                for i in range(8):
                    tile = update[p * 64 + i * 8 : p * 64 + i * 8 + 8, u * LANES : (u + 1) * LANES]
                    wide[place(i * 8, p + 1, c), :] = tile
                    if p == 15 and i < 7:
                        wide[place(i * 8 + 8, 0, c), :] = tile
                    if p == 0 and i > 0:
                        wide[place(i * 8 - 8, EXT - 1, c), :] = tile

    narrow(wide, out_ref)


def shuffled_attention(b, x, gain, shift, wqkv, wproj, bias):
    return pl.pallas_call(
        functools.partial(shuffled_kernel, b),
        out_shape=jax.ShapeDtypeStruct((COLS * STRIDE, LANES), BF),
        in_specs=[VM, VM, VM, ANY, ANY, VM],
        out_specs=VM,
        scratch_shapes=[pltpu.VMEM((COLS * STRIDE, LANES), F32), pltpu.VMEM((T, D), BF)]
        + ATTENTION_SCRATCH,
        compiler_params=pltpu.CompilerParams(vmem_limit_bytes=48 * 2**20),
        name="shuffled_attention",
    )(
        x,
        gain,
        shift,
        pltpu.with_memory_space_constraint(wqkv, pltpu.HBM),
        pltpu.with_memory_space_constraint(wproj, pltpu.HBM),
        bias,
    )


def tap_total(load, low, high, row, taps):
    total = None
    for step in range(3):
        source = row + step - 1
        if low <= source < high:
            for col in range(3):
                term = taps[3 * step + col] * load(source, col)
                total = term if total is None else total + term
    return total


def tap_rows(taps_ref, b, lanes):
    taps = [taps_ref[b, t : t + 1, lanes] for t in range(9)]
    taps[4] = taps[4] + 1.0
    return taps


def position():
    return lax.axis_index("pairs") * 2 + lax.axis_index("core")


def spread_kernel(b, x_ref, edge_ref, taps_ref, bias_ref, out_ref, wide, near):
    inner = jnp.where(position() == 0, 0.0, 1.0)
    slot = lax.broadcasted_iota(jnp.int32, (8, LANES), 0)

    @pl.loop(0, CHUNKS)
    def _(c):
        lanes = pl.ds(pl.multiple_of(c * LANES, LANES), LANES)
        taps = tap_rows(taps_ref, b, lanes)
        bias = bias_ref[b : b + 1, lanes]
        halo = [edge_ref[side, :, lanes].astype(F32) for side in range(2)]
        for r in range(ROWS):
            for side in range(2):
                near[r * PITCH + 6 + side : r * PITCH + 7 + side, :] = halo[side][r : r + 1]
            near[r * PITCH + 8 : r * PITCH + 8 + COLS, :] = x_ref[r, :, lanes].astype(F32)
        for i in range(8):
            loaded = {}

            def load(r, col):
                if (r, col) not in loaded:
                    start = r * PITCH + 6 + col + i * 8
                    x = near[start : start + 8, :]
                    if i == 0 and col != 1:
                        x = jnp.where(slot == 1 - col // 2, x * inner, x)
                    loaded[r, col] = x
                return loaded[r, col]

            for row in range(-1, ROWS + 1):
                total = tap_total(load, 0, ROWS, row, taps)
                wide[place(i * 8, row + 1, c), :] = total + bias if 0 <= row < ROWS else total

    narrow(wide, out_ref)


def spread_convolution(b, x, edge, taps, bias):
    return pl.pallas_call(
        functools.partial(spread_kernel, b),
        out_shape=jax.ShapeDtypeStruct((COLS * STRIDE, LANES), BF),
        in_specs=[VM] * 4,
        out_specs=VM,
        scratch_shapes=[
            pltpu.VMEM((COLS * STRIDE, LANES), F32),
            pltpu.VMEM((ROWS * PITCH, LANES), F32),
        ],
        compiler_params=pltpu.CompilerParams(vmem_limit_bytes=24 * 2**20),
        name="spread_convolution",
    )(x, edge, taps, bias)


def final_kernel(b, in_ref, edge_ref, taps_ref, bias_ref, out_ref, wide, near, held, sems):
    inner = jnp.where(position() == 0, 0.0, 1.0)
    outer = jnp.where(position() == 15, 0.0, 1.0)
    def piece(c):
        lanes = pl.ds(pl.multiple_of(c * LANES, LANES), LANES)
        return pltpu.make_async_copy(held.at[:, :, lanes], out_ref.at[:, :, lanes], sems.at[c])

    widen(in_ref, wide)
    end = COLS * STRIDE
    wide[:STRIDE, :] = wide[:STRIDE, :] * inner
    wide[end : end + STRIDE, :] = edge_ref[:STRIDE, :].astype(F32)
    wide[end + STRIDE :, :] = edge_ref[STRIDE:, :].astype(F32) * outer

    @pl.loop(0, CHUNKS)
    def _(c):
        lanes = pl.ds(pl.multiple_of(c * LANES, LANES), LANES)
        taps = tap_rows(taps_ref, b, lanes)
        bias = bias_ref[b : b + 1, lanes]
        for r in range(EXT):
            for i in range(8):
                near[r * PITCH + i * 8 : r * PITCH + i * 8 + 8, :] = wide[place(i * 8, r, c), :]
            for side in range(2):
                k = COLS + side
                at = k * STRIDE + r * CHUNKS + c
                near[r * PITCH + k : r * PITCH + k + 1, :] = wide[pl.ds(at, 1), :]
        for i in range(0, 8, 2):
            loaded = {}

            def load(r, col):
                if (r, col) not in loaded:
                    start = r * PITCH + i * 8 + col
                    loaded[r, col] = near[start : start + 16, :]
                return loaded[r, col]

            for row in range(ROWS):
                total = tap_total(load, 0, EXT, row + 1, taps) + bias
                held[row, i * 8 : i * 8 + 16, lanes] = total.astype(BF)
        piece(c).start()

    @pl.loop(0, CHUNKS)
    def _(c):
        piece(c).wait()

def final_convolution(b, x, edge, taps, bias):
    return pl.pallas_call(
        functools.partial(final_kernel, b),
        out_shape=jax.ShapeDtypeStruct((ROWS, COLS, D), BF),
        in_specs=[VM] * 4,
        out_specs=ANY,
        scratch_shapes=[
            pltpu.VMEM(((COLS + 2) * STRIDE, LANES), F32),
            pltpu.VMEM((EXT * PITCH, LANES), F32),
            pltpu.VMEM((ROWS, COLS, D), BF),
            pltpu.SemaphoreType.DMA((CHUNKS,)),
        ],
        compiler_params=pltpu.CompilerParams(vmem_limit_bytes=24 * 2**20),
        name="final_convolution",
    )(x, edge, taps, bias)


def shifted(columns, step):
    axes = ("pairs", "core")
    count = lax.axis_size(axes)
    return lax.ppermute(columns, axes, [(i, (i + step) % count) for i in range(count)])


def exchange(flat):
    blocks = flat.reshape(COLS, STRIDE, LANES)
    return lax.all_to_all(blocks, ("rows", "pairs"), split_axis=0, concat_axis=0, tiled=True)


def body(patches, gain, shift, wqkv, wproj, bias, taps, conv_bias):
    block_one, edge = local_attention(0, patches, gain, shift, wqkv, wproj, bias)
    outgoing = spread_convolution(0, block_one, shifted(edge, 1), taps, conv_bias)
    arrived = exchange(outgoing).reshape(COLS * STRIDE, LANES)
    returning = shuffled_attention(1, arrived, gain, shift, wqkv, wproj, bias)
    restored = exchange(returning).reshape(COLS * STRIDE, LANES)
    edge = shifted(restored[: 2 * STRIDE], -1)
    return final_convolution(1, restored, edge, taps, conv_bias)


def solution(mesh):
    grid = Mesh(mesh.devices.reshape(8, 8, 2), ("rows", "pairs", "core"))
    split = P("rows", ("pairs", "core"), None)
    return jax.shard_map(
        body,
        mesh=grid,
        in_specs=(split, P(), P(), P(), P(), P(), P(), P()),
        out_specs=split,
        check_vma=False,
    )
```

```python
import functools

import jax
import jax.numpy as jnp
from jax import lax
from jax.experimental import pallas as pl
from jax.experimental.pallas import tpu as pltpu
from jax.sharding import Mesh
from jax.sharding import PartitionSpec as P

BF = jnp.bfloat16
F32 = jnp.float32
D = 1024
T = 1024
NC = 1024
ROWS, COLS = 16, 64
EXT = ROWS + 2
LANES = 128
CHUNKS = D // LANES
STRIDE = EXT * CHUNKS
PITCH = (ROWS + 1) * CHUNKS

VM = pl.BlockSpec(memory_space=pltpu.VMEM)
ANY = pl.BlockSpec(memory_space=pl.ANY)


def normalise(x, gain, shift):
    center = x - jnp.mean(x, axis=-1, keepdims=True)
    spread = jnp.mean(center * center, axis=-1, keepdims=True)
    return (center * lax.rsqrt(spread + 1e-05) * gain + shift).astype(BF)


def attend_windows(first, count, packed, attended):
    lane = lax.broadcasted_iota(jnp.int32, (64, 256), 1) // 64
    masks = [jnp.where(lane == h, 0.125, 0.0).astype(BF) for h in range(4)]
    low = lax.broadcasted_iota(jnp.int32, (64, 128), 1) < 64
    units = [
        (pl.ds(pl.multiple_of((first + i) * 64, 64), 64), g)
        for i in range(count)
        for g in range(4)
    ]
    scores = []
    for rows, g in units:
        q = packed[rows, g * 256 : (g + 1) * 256]
        k = packed[rows, D + g * 256 : D + (g + 1) * 256]
        spread = jnp.concatenate([q * mask for mask in masks], axis=0)
        scores.append(
            lax.dot_general(k, spread, (((1,), (1,)), ((), ())), preferred_element_type=F32)
        )
    probabilities = []
    for s in scores:
        e = jnp.exp(s - jnp.max(s, axis=0, keepdims=True))
        probabilities.append((e * (1.0 / jnp.sum(e, axis=0, keepdims=True))).astype(BF))
    for (rows, g), p in zip(units, probabilities):
        v = packed[rows, 2 * D + g * 256 : 2 * D + (g + 1) * 256]
        for u in range(2):
            half = slice(u * 128, (u + 1) * 128)
            o = lax.dot_general(
                p[:, half], v[:, half], (((0,), (0,)), ((), ())), preferred_element_type=F32
            )
            start = g * 256 + u * 128
            attended[rows, start : start + 128] = jnp.where(low, o[:64], o[64:]).astype(BF)


def weight_copies(b, wqkv_hbm, wproj_hbm, wqkv, wproj, sems, psem):
    def piece(n):
        cols = pl.ds(pl.multiple_of(n * NC, NC), NC)
        return pltpu.make_async_copy(wqkv_hbm.at[b, :, cols], wqkv.at[:, cols], sems.at[n])

    return piece, pltpu.make_async_copy(wproj_hbm.at[b], wproj, psem)


def project_and_attend(piece, last, wqkv, normed, packed, attended):
    @pl.loop(0, 3 * D // NC)
    def _(n):
        piece(n).wait()
        cols = pl.ds(pl.multiple_of(n * NC, NC), NC)
        packed[:, cols] = jnp.dot(
            normed[...], wqkv[:, cols], preferred_element_type=F32
        ).astype(BF)

    @pl.loop(0, 2)
    def _(w):
        attend_windows(w * 8, 8, packed, attended)

    last.wait()


def local_kernel(
    b, x_hbm, gain_hbm, shift_hbm, wqkv_hbm, wproj_hbm, bias_hbm, out_ref, edge_ref,
    x_ref, gain, shift, bias, xsems, vsems, wqkv, wproj, normed, packed, attended, sems, psem,
):
    piece, last = weight_copies(b, wqkv_hbm, wproj_hbm, wqkv, wproj, sems, psem)
    vectors = [
        pltpu.make_async_copy(source, target, vsems.at[n])
        for n, (source, target) in enumerate(
            [(gain_hbm, gain), (shift_hbm, shift), (bias_hbm, bias)]
        )
    ]

    def tile(t):
        high = pl.ds(t // 4 * 8, 8)
        wide = pl.ds(pl.multiple_of(t % 4 * 16, 16), 16)
        return pltpu.make_async_copy(x_hbm.at[high, wide], x_ref.at[high, wide], xsems.at[t])

    for copy in vectors:
        copy.start()
    for t in range(8):
        tile(t).start()
    for copy in vectors:
        copy.wait()

    def norm(t):
        tile(t).wait()
        x = x_ref[pl.ds(t // 4 * 8, 8), pl.ds(pl.multiple_of(t % 4 * 16, 16), 16), :]
        x = x.astype(F32).reshape(8, 2, 8, D)
        for s in range(2):
            normed[pl.ds(pl.multiple_of(t * 128 + s * 64, 64), 64), :] = normalise(
                x[:, s].reshape(64, D), gain[b : b + 1], shift[b : b + 1]
            )

    pl.loop(0, 2, unroll=2)(norm)
    for n in range(3 * D // NC):
        piece(n).start()
    last.start()
    pl.loop(2, 8, unroll=6)(norm)

    project_and_attend(piece, last, wqkv, normed, packed, attended)

    @pl.loop(0, D // NC)
    def _(n):
        cols = pl.ds(pl.multiple_of(n * NC, NC), NC)
        update = jnp.dot(attended[...], wproj[:, cols], preferred_element_type=F32)
        update = update + bias[b : b + 1, cols]
        for t in range(8):
            high, wide = slice(t // 4 * 8, t // 4 * 8 + 8), slice(t % 4 * 16, t % 4 * 16 + 16)
            x = x_ref[high, wide, cols].astype(F32).reshape(8, 2, 8, NC)
            for s in range(2):
                for r in range(8):
                    at = t * 128 + s * 64 + r * 8
                    tile = update[at : at + 8] + x[r, s]
                    for c in range(CHUNKS):
                        start = (t % 4 * 16 + s * 8) * PITCH + (t // 4 * 8 + r) * CHUNKS + c
                        part = tile[:, c * LANES : (c + 1) * LANES]
                        out_ref[pl.ds(start, 8, stride=PITCH), :] = part

    for side in range(2):
        start = (COLS - 2 + side) * PITCH
        column = out_ref[start : start + ROWS * CHUNKS, :]
        edge_ref[side * ROWS * CHUNKS : (side + 1) * ROWS * CHUNKS, :] = column.astype(BF)


ATTENTION_SCRATCH = [
    pltpu.VMEM((D, 3 * D), BF),
    pltpu.VMEM((D, D), BF),
    pltpu.VMEM((T, D), BF),
    pltpu.VMEM((T, 3 * D), BF),
    pltpu.VMEM((T, D), BF),
    pltpu.SemaphoreType.DMA((3 * D // NC,)),
    pltpu.SemaphoreType.DMA,
]


def local_attention(b, x, gain, shift, wqkv, wproj, bias):
    edge = jax.ShapeDtypeStruct((2 * ROWS * CHUNKS, LANES), BF)
    x, gain, shift, wqkv, wproj, bias = [
        pltpu.with_memory_space_constraint(a, pltpu.HBM)
        for a in (x, gain, shift, wqkv, wproj, bias)
    ]
    return pl.pallas_call(
        functools.partial(local_kernel, b),
        out_shape=(jax.ShapeDtypeStruct((COLS * PITCH, LANES), F32), edge),
        in_specs=[ANY] * 6,
        out_specs=(VM, VM),
        scratch_shapes=[
            pltpu.VMEM((ROWS, COLS, D), BF),
            pltpu.VMEM((2, D), F32),
            pltpu.VMEM((2, D), F32),
            pltpu.VMEM((2, D), F32),
            pltpu.SemaphoreType.DMA((8,)),
            pltpu.SemaphoreType.DMA((3,)),
        ]
        + ATTENTION_SCRATCH,
        compiler_params=pltpu.CompilerParams(vmem_limit_bytes=40 * 2**20),
        name="local_attention",
    )(x, gain, shift, wqkv, wproj, bias)


def place(col, row, chunk):
    return pl.ds(col * STRIDE + row * CHUNKS + chunk, 8, stride=STRIDE)


def widen(flat, wide):
    @pl.loop(0, 16)
    def _(n):
        rows = pl.ds(pl.multiple_of(n * 576, 576), 576)
        wide[rows, :] = flat[rows, :].astype(F32)


def narrow(wide, flat):
    @pl.loop(0, 16)
    def _(n):
        rows = pl.ds(pl.multiple_of(n * 576, 576), 576)
        flat[rows, :] = wide[rows, :].astype(BF)


def shuffled_kernel(
    b, in_ref, gain, shift, wqkv_hbm, wproj_hbm, bias, out_ref,
    wide, stream, wqkv, wproj, normed, packed, attended, sems, psem,
):
    piece, last = weight_copies(b, wqkv_hbm, wproj_hbm, wqkv, wproj, sems, psem)
    for n in range(3 * D // NC):
        piece(n).start()
    last.start()
    widen(in_ref, wide)

    @pl.loop(0, CHUNKS)
    def _(c):
        for i in range(7):
            above, below = i * 8, (i + 1) * 8
            wide[place(below, 1, c), :] += wide[place(above, EXT - 1, c), :]
            wide[place(above, EXT - 2, c), :] += wide[place(below, 0, c), :]

    @pl.loop(0, 16, unroll=4)
    def _(p):
        x = jnp.concatenate(
            [
                jnp.concatenate([wide[place(i * 8, p + 1, c), :] for c in range(CHUNKS)], axis=1)
                for i in range(8)
            ],
            axis=0,
        ).astype(BF)
        rows = pl.ds(pl.multiple_of(p * 64, 64), 64)
        stream[rows, :] = x
        normed[rows, :] = normalise(x.astype(F32), gain[b : b + 1], shift[b : b + 1])

    project_and_attend(piece, last, wqkv, normed, packed, attended)

    @pl.loop(0, D // NC)
    def _(n):
        cols = pl.ds(pl.multiple_of(n * NC, NC), NC)
        update = jnp.dot(attended[...], wproj[:, cols], preferred_element_type=F32)
        update = update + bias[b : b + 1, cols] + stream[:, cols].astype(F32)
        for u in range(NC // LANES):
            c = n * (NC // LANES) + u
            wide[place(0, 0, c), :] = jnp.zeros((8, LANES), F32)
            wide[place(56, EXT - 1, c), :] = jnp.zeros((8, LANES), F32)
            for p in range(16):
                for i in range(8):
                    tile = update[p * 64 + i * 8 : p * 64 + i * 8 + 8, u * LANES : (u + 1) * LANES]
                    wide[place(i * 8, p + 1, c), :] = tile
                    if p == 15 and i < 7:
                        wide[place(i * 8 + 8, 0, c), :] = tile
                    if p == 0 and i > 0:
                        wide[place(i * 8 - 8, EXT - 1, c), :] = tile

    narrow(wide, out_ref)


def shuffled_attention(b, x, gain, shift, wqkv, wproj, bias):
    return pl.pallas_call(
        functools.partial(shuffled_kernel, b),
        out_shape=jax.ShapeDtypeStruct((COLS * STRIDE, LANES), BF),
        in_specs=[VM, VM, VM, ANY, ANY, VM],
        out_specs=VM,
        scratch_shapes=[pltpu.VMEM((COLS * STRIDE, LANES), F32), pltpu.VMEM((T, D), BF)]
        + ATTENTION_SCRATCH,
        compiler_params=pltpu.CompilerParams(vmem_limit_bytes=48 * 2**20),
        name="shuffled_attention",
    )(
        x,
        gain,
        shift,
        pltpu.with_memory_space_constraint(wqkv, pltpu.HBM),
        pltpu.with_memory_space_constraint(wproj, pltpu.HBM),
        bias,
    )


def stage_taps(taps_ref, bias_ref, b, tiles):
    for c in range(CHUNKS):
        lanes = slice(c * LANES, (c + 1) * LANES)
        for t in range(9):
            tap = taps_ref[b, t : t + 1, lanes]
            tiles[t * 8 + c : t * 8 + c + 1, :] = tap + 1.0 if t == 4 else tap
        tiles[72 + c : 73 + c, :] = bias_ref[b : b + 1, lanes]


def column_sums(load, rows, low, high, taps):
    loaded = {}
    sums = []
    for row in rows:
        total = None
        for step in range(3):
            source = row + step - 1
            if low <= source < high:
                for col in range(3):
                    if (source, col) not in loaded:
                        loaded[source, col] = load(source, col)
                    term = taps[3 * step + col] * loaded[source, col]
                    total = term if total is None else total + term
        sums.append(total)
    return sums


def position():
    return lax.axis_index("pairs") * 2 + lax.axis_index("core")


def spread_kernel(b, x_ref, edge_ref, taps_ref, bias_ref, out_ref, edge, tiles):
    inner = jnp.where(position() == 0, 0.0, 1.0)
    stage_taps(taps_ref, bias_ref, b, tiles)
    edge[...] = edge_ref[...].astype(F32)

    def column(k, scales=(None, None, None)):
        taps = []
        for t in range(9):
            tap = tiles[t * 8 : t * 8 + 8, :]
            taps.append(tap if scales[t % 3] is None else tap * scales[t % 3])
        bias = tiles[72:80, :]

        def load(r, col):
            if isinstance(k, int) and k + col < 2:
                start = ((k + col) * ROWS + r) * CHUNKS
                return edge[start : start + 8, :]
            return x_ref[pl.ds(pl.multiple_of((k + col - 2) * PITCH + r * 8, 8), 8), :]

        sums = column_sums(load, range(-1, ROWS + 1), 0, ROWS, taps)
        sums[1:-1] = [total + bias for total in sums[1:-1]]
        for pair in range(EXT // 2):
            rows = pl.ds(pl.multiple_of(k * STRIDE + pair * 16, 16), 16)
            both = jnp.concatenate(sums[2 * pair : 2 * pair + 2], axis=0)
            out_ref[rows, :] = both.astype(BF)

    column(0, (None, None, inner))
    column(1, (inner, None, None))

    @pl.loop(2, COLS, unroll=2)
    def _(k):
        column(k)


def spread_convolution(b, x, edge, taps, bias):
    return pl.pallas_call(
        functools.partial(spread_kernel, b),
        out_shape=jax.ShapeDtypeStruct((COLS * STRIDE, LANES), BF),
        in_specs=[VM] * 4,
        out_specs=VM,
        scratch_shapes=[
            pltpu.VMEM((2 * ROWS * CHUNKS, LANES), F32),
            pltpu.VMEM((80, LANES), F32),
        ],
        compiler_params=pltpu.CompilerParams(vmem_limit_bytes=24 * 2**20),
        name="spread_convolution",
    )(x, edge, taps, bias)


def final_kernel(
    b, in_ref, edge_ref, taps_ref, bias_ref, out_ref, wide, natural, held, tiles, sems
):
    inner = jnp.where(position() == 0, 0.0, 1.0)
    outer = jnp.where(position() == 15, 0.0, 1.0)

    def piece(n):
        cols = pl.ds(pl.multiple_of(n * 16, 16), 16)
        return pltpu.make_async_copy(held.at[:, cols], out_ref.at[:, cols], sems.at[n])

    stage_taps(taps_ref, bias_ref, b, tiles)
    widen(in_ref, wide)
    end = COLS * STRIDE
    wide[:STRIDE, :] = wide[:STRIDE, :] * inner
    wide[end : end + STRIDE, :] = edge_ref[:STRIDE, :].astype(F32)
    wide[end + STRIDE :, :] = edge_ref[STRIDE:, :].astype(F32) * outer

    @pl.loop(0, COLS // 16)
    def _(n):
        @pl.loop(0, 16, unroll=4)
        def _(w):
            taps = [tiles[t * 8 : t * 8 + 8, :] for t in range(9)]
            bias = tiles[72:80, :]

            def load(r, col):
                start = (n * 16 + w + col) * STRIDE + r * 8
                return wide[pl.ds(pl.multiple_of(start, 8), 8), :]

            sums = column_sums(load, range(1, EXT - 1), 0, EXT, taps)
            for row in range(ROWS):
                start = row * 128 + w // 8 * 64 + w % 8
                natural[pl.ds(start, 8, stride=8), :] = sums[row] + bias

        for row in range(ROWS):
            for c in range(CHUNKS):
                start = row * 128 + c * 8
                both = jnp.concatenate(
                    [natural[start : start + 8, :], natural[start + 64 : start + 72, :]], axis=0
                )
                cols = pl.ds(pl.multiple_of(n * 16, 16), 16)
                held[row, cols, c * LANES : (c + 1) * LANES] = both.astype(BF)
        piece(n).start()

    @pl.loop(0, COLS // 16)
    def _(n):
        piece(n).wait()


def final_convolution(b, x, edge, taps, bias):
    return pl.pallas_call(
        functools.partial(final_kernel, b),
        out_shape=jax.ShapeDtypeStruct((ROWS, COLS, D), BF),
        in_specs=[VM] * 4,
        out_specs=ANY,
        scratch_shapes=[
            pltpu.VMEM(((COLS + 2) * STRIDE, LANES), F32),
            pltpu.VMEM((ROWS * 128, LANES), F32),
            pltpu.VMEM((ROWS, COLS, D), BF),
            pltpu.VMEM((80, LANES), F32),
            pltpu.SemaphoreType.DMA((COLS // 16,)),
        ],
        compiler_params=pltpu.CompilerParams(vmem_limit_bytes=24 * 2**20),
        name="final_convolution",
    )(x, edge, taps, bias)


def shifted(columns, step):
    axes = ("pairs", "core")
    count = lax.axis_size(axes)
    return lax.ppermute(columns, axes, [(i, (i + step) % count) for i in range(count)])


def exchange(flat):
    blocks = flat.reshape(COLS, STRIDE, LANES)
    return lax.all_to_all(blocks, ("rows", "pairs"), split_axis=0, concat_axis=0, tiled=True)


def body(patches, gain, shift, wqkv, wproj, bias, taps, conv_bias):
    block_one, edge = local_attention(0, patches, gain, shift, wqkv, wproj, bias)
    outgoing = spread_convolution(0, block_one, shifted(edge, 1), taps, conv_bias)
    arrived = exchange(outgoing).reshape(COLS * STRIDE, LANES)
    returning = shuffled_attention(1, arrived, gain, shift, wqkv, wproj, bias)
    restored = exchange(returning).reshape(COLS * STRIDE, LANES)
    edge = shifted(restored[: 2 * STRIDE], -1)
    return final_convolution(1, restored, edge, taps, conv_bias)


def solution(mesh):
    grid = Mesh(mesh.devices.reshape(8, 8, 2), ("rows", "pairs", "core"))
    split = P("rows", ("pairs", "core"), None)
    return jax.shard_map(
        body,
        mesh=grid,
        in_specs=(split, P(), P(), P(), P(), P(), P(), P()),
        out_specs=split,
        check_vma=False,
    )
```

```python
import functools

import jax
import jax.numpy as jnp
from jax import lax
from jax.experimental import pallas as pl
from jax.experimental.pallas import tpu as pltpu
from jax.sharding import Mesh
from jax.sharding import PartitionSpec as P

BF = jnp.bfloat16
F32 = jnp.float32
D = 1024
T = 1024
NC = 1024
ROWS, COLS = 16, 64
EXT = ROWS + 2
LANES = 128
CHUNKS = D // LANES
STRIDE = EXT * CHUNKS
PITCH = (ROWS + 1) * CHUNKS

VM = pl.BlockSpec(memory_space=pltpu.VMEM)
ANY = pl.BlockSpec(memory_space=pl.ANY)


def normalise(x, gain, shift):
    center = x - jnp.mean(x, axis=-1, keepdims=True)
    spread = jnp.mean(center * center, axis=-1, keepdims=True)
    return (center * lax.rsqrt(spread + 1e-05) * gain + shift).astype(BF)


def attend_windows(first, count, packed, attended):
    lane = lax.broadcasted_iota(jnp.int32, (64, 256), 1) // 64
    masks = [jnp.where(lane == h, 0.125, 0.0).astype(BF) for h in range(4)]
    low = lax.broadcasted_iota(jnp.int32, (64, 128), 1) < 64
    units = [
        (pl.ds(pl.multiple_of((first + i) * 64, 64), 64), g)
        for i in range(count)
        for g in range(4)
    ]
    scores = []
    for rows, g in units:
        q = packed[rows, g * 256 : (g + 1) * 256]
        k = packed[rows, D + g * 256 : D + (g + 1) * 256]
        spread = jnp.concatenate([q * mask for mask in masks], axis=0)
        scores.append(
            lax.dot_general(k, spread, (((1,), (1,)), ((), ())), preferred_element_type=F32)
        )
    probabilities = []
    for s in scores:
        e = jnp.exp(s - jnp.max(s, axis=0, keepdims=True))
        probabilities.append((e * (1.0 / jnp.sum(e, axis=0, keepdims=True))).astype(BF))
    for (rows, g), p in zip(units, probabilities):
        v = packed[rows, 2 * D + g * 256 : 2 * D + (g + 1) * 256]
        for u in range(2):
            half = slice(u * 128, (u + 1) * 128)
            o = lax.dot_general(
                p[:, half], v[:, half], (((0,), (0,)), ((), ())), preferred_element_type=F32
            )
            start = g * 256 + u * 128
            attended[rows, start : start + 128] = jnp.where(low, o[:64], o[64:]).astype(BF)


def weight_copies(b, wqkv_hbm, wproj_hbm, wqkv, wproj, sems, psem):
    def piece(n):
        cols = pl.ds(pl.multiple_of(n * NC, NC), NC)
        return pltpu.make_async_copy(wqkv_hbm.at[b, :, cols], wqkv.at[:, cols], sems.at[n])

    return piece, pltpu.make_async_copy(wproj_hbm.at[b], wproj, psem)


def project_and_attend(pieces, piece, last, wqkv, normed, packed, attended):
    width = 3 * D // pieces

    @pl.loop(0, pieces)
    def _(n):
        for part in range(3 // pieces):
            piece(n * (3 // pieces) + part).wait()
        cols = pl.ds(pl.multiple_of(n * width, width), width)
        packed[:, cols] = jnp.dot(
            normed[...], wqkv[:, cols], preferred_element_type=F32
        ).astype(BF)

    @pl.loop(0, 2)
    def _(w):
        attend_windows(w * 8, 8, packed, attended)

    last.wait()


def local_kernel(
    b, x_hbm, gain_hbm, shift_hbm, wqkv_hbm, wproj_hbm, bias_hbm, out_ref, edge_ref,
    x_ref, gain, shift, bias, xsems, vsems, wqkv, wproj, normed, packed, attended, sems, psem,
):
    piece, last = weight_copies(b, wqkv_hbm, wproj_hbm, wqkv, wproj, sems, psem)
    vectors = [
        pltpu.make_async_copy(source, target, vsems.at[n])
        for n, (source, target) in enumerate(
            [(gain_hbm, gain), (shift_hbm, shift), (bias_hbm, bias)]
        )
    ]

    def tile(t):
        high = pl.ds(t // 4 * 8, 8)
        wide = pl.ds(pl.multiple_of(t % 4 * 16, 16), 16)
        return pltpu.make_async_copy(x_hbm.at[high, wide], x_ref.at[high, wide], xsems.at[t])

    for copy in vectors:
        copy.start()
    for t in range(8):
        tile(t).start()
    for copy in vectors:
        copy.wait()

    def norm(t):
        tile(t).wait()
        x = x_ref[pl.ds(t // 4 * 8, 8), pl.ds(pl.multiple_of(t % 4 * 16, 16), 16), :]
        x = x.astype(F32).reshape(8, 2, 8, D)
        for s in range(2):
            normed[pl.ds(pl.multiple_of(t * 128 + s * 64, 64), 64), :] = normalise(
                x[:, s].reshape(64, D), gain[b : b + 1], shift[b : b + 1]
            )

    pl.loop(0, 2, unroll=2)(norm)
    for n in range(3 * D // NC):
        piece(n).start()
    last.start()
    pl.loop(2, 8, unroll=6)(norm)

    project_and_attend(3, piece, last, wqkv, normed, packed, attended)

    @pl.loop(0, D // NC)
    def _(n):
        cols = pl.ds(pl.multiple_of(n * NC, NC), NC)
        update = jnp.dot(attended[...], wproj[:, cols], preferred_element_type=F32)
        update = update + bias[b : b + 1, cols]
        for t in range(8):
            high, wide = slice(t // 4 * 8, t // 4 * 8 + 8), slice(t % 4 * 16, t % 4 * 16 + 16)
            x = x_ref[high, wide, cols].astype(F32).reshape(8, 2, 8, NC)
            for s in range(2):
                for r in range(8):
                    at = t * 128 + s * 64 + r * 8
                    tile = update[at : at + 8] + x[r, s]
                    for c in range(CHUNKS):
                        start = (t % 4 * 16 + s * 8) * PITCH + (t // 4 * 8 + r) * CHUNKS + c
                        part = tile[:, c * LANES : (c + 1) * LANES]
                        out_ref[pl.ds(start, 8, stride=PITCH), :] = part

    for side in range(2):
        start = (COLS - 2 + side) * PITCH
        column = out_ref[start : start + ROWS * CHUNKS, :]
        edge_ref[side * ROWS * CHUNKS : (side + 1) * ROWS * CHUNKS, :] = column.astype(BF)


ATTENTION_SCRATCH = [
    pltpu.VMEM((D, 3 * D), BF),
    pltpu.VMEM((D, D), BF),
    pltpu.VMEM((T, D), BF),
    pltpu.VMEM((T, 3 * D), BF),
    pltpu.VMEM((T, D), BF),
    pltpu.SemaphoreType.DMA((3 * D // NC,)),
    pltpu.SemaphoreType.DMA,
]


def local_attention(b, x, gain, shift, wqkv, wproj, bias):
    edge = jax.ShapeDtypeStruct((2 * ROWS * CHUNKS, LANES), BF)
    x, gain, shift, wqkv, wproj, bias = [
        pltpu.with_memory_space_constraint(a, pltpu.HBM)
        for a in (x, gain, shift, wqkv, wproj, bias)
    ]
    return pl.pallas_call(
        functools.partial(local_kernel, b),
        out_shape=(jax.ShapeDtypeStruct((COLS * PITCH, LANES), F32), edge),
        in_specs=[ANY] * 6,
        out_specs=(VM, VM),
        scratch_shapes=[
            pltpu.VMEM((ROWS, COLS, D), BF),
            pltpu.VMEM((2, D), F32),
            pltpu.VMEM((2, D), F32),
            pltpu.VMEM((2, D), F32),
            pltpu.SemaphoreType.DMA((8,)),
            pltpu.SemaphoreType.DMA((3,)),
        ]
        + ATTENTION_SCRATCH,
        compiler_params=pltpu.CompilerParams(vmem_limit_bytes=40 * 2**20),
        name="local_attention",
    )(x, gain, shift, wqkv, wproj, bias)


def place(col, row, chunk):
    return pl.ds(col * STRIDE + row * CHUNKS + chunk, 8, stride=STRIDE)


def widen(flat, wide):
    @pl.loop(0, 16)
    def _(n):
        rows = pl.ds(pl.multiple_of(n * 576, 576), 576)
        wide[rows, :] = flat[rows, :].astype(F32)


def narrow(wide, flat):
    @pl.loop(0, 16)
    def _(n):
        rows = pl.ds(pl.multiple_of(n * 576, 576), 576)
        flat[rows, :] = wide[rows, :].astype(BF)


def shuffled_kernel(
    b, in_ref, gain, shift, wqkv_hbm, wproj_hbm, bias, out_ref,
    wide, stream, wqkv, wproj, normed, packed, attended, sems, psem,
):
    piece, last = weight_copies(b, wqkv_hbm, wproj_hbm, wqkv, wproj, sems, psem)
    for n in range(3 * D // NC):
        piece(n).start()
    last.start()
    widen(in_ref, wide)

    @pl.loop(0, CHUNKS)
    def _(c):
        for i in range(7):
            above, below = i * 8, (i + 1) * 8
            wide[place(below, 1, c), :] += wide[place(above, EXT - 1, c), :]
            wide[place(above, EXT - 2, c), :] += wide[place(below, 0, c), :]

    @pl.loop(0, 16, unroll=4)
    def _(p):
        x = jnp.concatenate(
            [
                jnp.concatenate([wide[place(i * 8, p + 1, c), :] for c in range(CHUNKS)], axis=1)
                for i in range(8)
            ],
            axis=0,
        ).astype(BF)
        rows = pl.ds(pl.multiple_of(p * 64, 64), 64)
        stream[rows, :] = x
        normed[rows, :] = normalise(x.astype(F32), gain[b : b + 1], shift[b : b + 1])

    project_and_attend(1, piece, last, wqkv, normed, packed, attended)

    @pl.loop(0, D // NC)
    def _(n):
        cols = pl.ds(pl.multiple_of(n * NC, NC), NC)
        update = jnp.dot(attended[...], wproj[:, cols], preferred_element_type=F32)
        update = update + bias[b : b + 1, cols] + stream[:, cols].astype(F32)
        for u in range(NC // LANES):
            c = n * (NC // LANES) + u
            wide[place(0, 0, c), :] = jnp.zeros((8, LANES), F32)
            wide[place(56, EXT - 1, c), :] = jnp.zeros((8, LANES), F32)
            for p in range(16):
                for i in range(8):
                    tile = update[p * 64 + i * 8 : p * 64 + i * 8 + 8, u * LANES : (u + 1) * LANES]
                    wide[place(i * 8, p + 1, c), :] = tile
                    if p == 15 and i < 7:
                        wide[place(i * 8 + 8, 0, c), :] = tile
                    if p == 0 and i > 0:
                        wide[place(i * 8 - 8, EXT - 1, c), :] = tile

    narrow(wide, out_ref)


def shuffled_attention(b, x, gain, shift, wqkv, wproj, bias):
    return pl.pallas_call(
        functools.partial(shuffled_kernel, b),
        out_shape=jax.ShapeDtypeStruct((COLS * STRIDE, LANES), BF),
        in_specs=[VM, VM, VM, ANY, ANY, VM],
        out_specs=VM,
        scratch_shapes=[pltpu.VMEM((COLS * STRIDE, LANES), F32), pltpu.VMEM((T, D), BF)]
        + ATTENTION_SCRATCH,
        compiler_params=pltpu.CompilerParams(vmem_limit_bytes=48 * 2**20),
        name="shuffled_attention",
    )(
        x,
        gain,
        shift,
        pltpu.with_memory_space_constraint(wqkv, pltpu.HBM),
        pltpu.with_memory_space_constraint(wproj, pltpu.HBM),
        bias,
    )


def stage_taps(taps_ref, bias_ref, b, tiles):
    for c in range(CHUNKS):
        lanes = slice(c * LANES, (c + 1) * LANES)
        for t in range(9):
            tap = taps_ref[b, t : t + 1, lanes]
            tiles[t * 8 + c : t * 8 + c + 1, :] = tap + 1.0 if t == 4 else tap
        tiles[72 + c : 73 + c, :] = bias_ref[b : b + 1, lanes]


def column_sums(load, rows, low, high, taps):
    loaded = {}
    sums = []
    for row in rows:
        total = None
        for step in range(3):
            source = row + step - 1
            if low <= source < high:
                for col in range(3):
                    if (source, col) not in loaded:
                        loaded[source, col] = load(source, col)
                    term = taps[3 * step + col] * loaded[source, col]
                    total = term if total is None else total + term
        sums.append(total)
    return sums


def position():
    return lax.axis_index("pairs") * 2 + lax.axis_index("core")


def spread_column(k, load, tiles, out_ref, scales=(None, None, None)):
    taps = []
    for t in range(9):
        tap = tiles[t * 8 : t * 8 + 8, :]
        taps.append(tap if scales[t % 3] is None else tap * scales[t % 3])
    bias = tiles[72:80, :]
    sums = column_sums(load, range(-1, ROWS + 1), 0, ROWS, taps)
    sums[1:-1] = [total + bias for total in sums[1:-1]]
    for pair in range(EXT // 2):
        rows = pl.ds(pl.multiple_of(k * STRIDE + pair * 16, 16), 16)
        both = jnp.concatenate(sums[2 * pair : 2 * pair + 2], axis=0)
        out_ref[rows, :] = both.astype(BF)


def inner_spread_kernel(b, x_ref, taps_ref, bias_ref, out_ref, tiles):
    stage_taps(taps_ref, bias_ref, b, tiles)

    @pl.loop(2, COLS, unroll=2)
    def _(k):
        def load(r, col):
            return x_ref[pl.ds(pl.multiple_of((k + col - 2) * PITCH + r * 8, 8), 8), :]

        spread_column(k, load, tiles, out_ref)


def outer_spread_kernel(
    b, x_ref, edge_ref, taps_ref, bias_ref, _, out_ref, edge, held, tiles, sem
):
    inner = jnp.where(position() == 0, 0.0, 1.0)
    stage_taps(taps_ref, bias_ref, b, tiles)
    edge[...] = edge_ref[...].astype(F32)
    for k, scales in enumerate([(None, None, inner), (inner, None, None)]):

        def load(r, col):
            if k + col < 2:
                start = ((k + col) * ROWS + r) * CHUNKS
                return edge[start : start + 8, :]
            start = (k + col - 2) * PITCH + r * 8
            return x_ref[start : start + 8, :]

        spread_column(k, load, tiles, held, scales)
    copy = pltpu.make_async_copy(held, out_ref.at[pl.ds(0, 2 * STRIDE)], sem)
    copy.start()
    copy.wait()


def spread_convolution(b, x, edge, taps, bias):
    out = jax.ShapeDtypeStruct((COLS * STRIDE, LANES), BF)
    params = pltpu.CompilerParams(vmem_limit_bytes=24 * 2**20)
    inner = pl.pallas_call(
        functools.partial(inner_spread_kernel, b),
        out_shape=out,
        in_specs=[VM] * 3,
        out_specs=VM,
        scratch_shapes=[pltpu.VMEM((80, LANES), F32)],
        compiler_params=params,
        cost_estimate=pl.CostEstimate(flops=10**9, bytes_accessed=10**7, transcendentals=0),
        name="inner_spread_convolution",
    )(x, taps, bias)
    return pl.pallas_call(
        functools.partial(outer_spread_kernel, b),
        out_shape=out,
        in_specs=[VM] * 4 + [ANY],
        out_specs=ANY,
        scratch_shapes=[
            pltpu.VMEM((2 * ROWS * CHUNKS, LANES), F32),
            pltpu.VMEM((2 * STRIDE, LANES), BF),
            pltpu.VMEM((80, LANES), F32),
            pltpu.SemaphoreType.DMA,
        ],
        input_output_aliases={4: 0},
        compiler_params=params,
        name="outer_spread_convolution",
    )(x, edge, taps, bias, inner)


FIRST = 48


def final_columns(b, low, high, load_from, masks, taps_ref, bias_ref, out_ref, scratch):
    wide, natural, held, tiles, sems = scratch
    inner, outer = masks

    def piece(n):
        cols = pl.ds(pl.multiple_of(low + n * 16, 16), 16)
        mine = pl.ds(pl.multiple_of(n * 16, 16), 16)
        return pltpu.make_async_copy(held.at[:, mine], out_ref.at[:, cols], sems.at[n])

    stage_taps(taps_ref, bias_ref, b, tiles)
    load_from(wide)
    if inner is not None:
        wide[:STRIDE, :] = wide[:STRIDE, :] * inner
    if outer is not None:
        end = (high - low + 1) * STRIDE
        wide[end : end + STRIDE, :] = wide[end : end + STRIDE, :] * outer

    @pl.loop(0, (high - low) // 16)
    def _(n):
        @pl.loop(0, 16, unroll=4)
        def _(w):
            taps = [tiles[t * 8 : t * 8 + 8, :] for t in range(9)]
            bias = tiles[72:80, :]

            def load(r, col):
                start = (n * 16 + w + col) * STRIDE + r * 8
                return wide[pl.ds(pl.multiple_of(start, 8), 8), :]

            sums = column_sums(load, range(1, EXT - 1), 0, EXT, taps)
            for row in range(ROWS):
                start = row * 128 + w // 8 * 64 + w % 8
                natural[pl.ds(start, 8, stride=8), :] = sums[row] + bias

        for row in range(ROWS):
            for c in range(CHUNKS):
                start = row * 128 + c * 8
                both = jnp.concatenate(
                    [natural[start : start + 8, :], natural[start + 64 : start + 72, :]], axis=0
                )
                cols = pl.ds(pl.multiple_of(n * 16, 16), 16)
                held[row, cols, c * LANES : (c + 1) * LANES] = both.astype(BF)
        piece(n).start()

    @pl.loop(0, (high - low) // 16)
    def _(n):
        piece(n).wait()


def first_final_kernel(b, in_ref, taps_ref, bias_ref, out_ref, *scratch):
    inner = jnp.where(position() == 0, 0.0, 1.0)

    def load_from(wide):
        @pl.loop(0, (FIRST + 2) // 2)
        def _(n):
            rows = pl.ds(pl.multiple_of(n * 2 * STRIDE, 2 * STRIDE), 2 * STRIDE)
            wide[rows, :] = in_ref[rows, :].astype(F32)

    final_columns(b, 0, FIRST, load_from, (inner, None), taps_ref, bias_ref, out_ref, scratch)


def second_final_kernel(b, in_ref, edge_ref, taps_ref, bias_ref, _, out_ref, *scratch):
    outer = jnp.where(position() == 15, 0.0, 1.0)
    count = (COLS - FIRST) * STRIDE

    def load_from(wide):
        wide[:count, :] = in_ref[FIRST * STRIDE :, :].astype(F32)
        wide[count:, :] = edge_ref[...].astype(F32)

    final_columns(b, FIRST, COLS, load_from, (None, outer), taps_ref, bias_ref, out_ref, scratch)


def final_scratch(columns):
    return [
        pltpu.VMEM(((columns + 2) * STRIDE, LANES), F32),
        pltpu.VMEM((ROWS * 128, LANES), F32),
        pltpu.VMEM((ROWS, columns, D), BF),
        pltpu.VMEM((80, LANES), F32),
        pltpu.SemaphoreType.DMA((columns // 16,)),
    ]


def final_convolution(b, x, edge, taps, bias):
    out = jax.ShapeDtypeStruct((ROWS, COLS, D), BF)
    params = pltpu.CompilerParams(vmem_limit_bytes=24 * 2**20)
    first = pl.pallas_call(
        functools.partial(first_final_kernel, b),
        out_shape=out,
        in_specs=[VM] * 3,
        out_specs=ANY,
        scratch_shapes=final_scratch(FIRST),
        compiler_params=params,
        cost_estimate=pl.CostEstimate(flops=10**9, bytes_accessed=10**7, transcendentals=0),
        name="first_final_convolution",
    )(x, taps, bias)
    return pl.pallas_call(
        functools.partial(second_final_kernel, b),
        out_shape=out,
        in_specs=[VM] * 4 + [ANY],
        out_specs=ANY,
        scratch_shapes=final_scratch(COLS - FIRST),
        input_output_aliases={4: 0},
        compiler_params=params,
        name="second_final_convolution",
    )(x, edge, taps, bias, first)


def shifted(columns, step):
    axes = ("pairs", "core")
    count = lax.axis_size(axes)
    return lax.ppermute(columns, axes, [(i, (i + step) % count) for i in range(count)])


def exchange(flat):
    blocks = flat.reshape(COLS, STRIDE, LANES)
    return lax.all_to_all(blocks, ("rows", "pairs"), split_axis=0, concat_axis=0, tiled=True)


def body(patches, gain, shift, wqkv, wproj, bias, taps, conv_bias):
    block_one, edge = local_attention(0, patches, gain, shift, wqkv, wproj, bias)
    outgoing = spread_convolution(0, block_one, shifted(edge, 1), taps, conv_bias)
    arrived = exchange(outgoing).reshape(COLS * STRIDE, LANES)
    returning = shuffled_attention(1, arrived, gain, shift, wqkv, wproj, bias)
    restored = exchange(returning).reshape(COLS * STRIDE, LANES)
    edge = shifted(restored[: 2 * STRIDE], -1)
    return final_convolution(1, restored, edge, taps, conv_bias)


def solution(mesh):
    grid = Mesh(mesh.devices.reshape(8, 8, 2), ("rows", "pairs", "core"))
    split = P("rows", ("pairs", "core"), None)
    return jax.shard_map(
        body,
        mesh=grid,
        in_specs=(split, P(), P(), P(), P(), P(), P(), P()),
        out_specs=split,
        check_vma=False,
    )
```

```python
import functools

import jax
import jax.numpy as jnp
from jax import lax
from jax.experimental import pallas as pl
from jax.experimental.pallas import tpu as pltpu
from jax.sharding import Mesh
from jax.sharding import PartitionSpec as P

BF = jnp.bfloat16
F32 = jnp.float32
D = 1024
T = 1024
NC = 1024
ROWS, COLS = 16, 64
EXT = ROWS + 2
LANES = 128
CHUNKS = D // LANES
STRIDE = EXT * CHUNKS
PITCH = (ROWS + 1) * CHUNKS

VM = pl.BlockSpec(memory_space=pltpu.VMEM)
ANY = pl.BlockSpec(memory_space=pl.ANY)


def normalise(x, gain, shift):
    center = x - jnp.mean(x, axis=-1, keepdims=True)
    spread = jnp.mean(center * center, axis=-1, keepdims=True)
    return (center * lax.rsqrt(spread + 1e-05) * gain + shift).astype(BF)


def attend_windows(first, count, packed, attended):
    lane = lax.broadcasted_iota(jnp.int32, (64, 256), 1) // 64
    masks = [jnp.where(lane == h, 0.125, 0.0).astype(BF) for h in range(4)]
    low = lax.broadcasted_iota(jnp.int32, (64, 128), 1) < 64
    units = [
        (pl.ds(pl.multiple_of((first + i) * 64, 64), 64), g)
        for i in range(count)
        for g in range(4)
    ]
    scores = []
    for rows, g in units:
        q = packed[rows, g * 256 : (g + 1) * 256]
        k = packed[rows, D + g * 256 : D + (g + 1) * 256]
        spread = jnp.concatenate([q * mask for mask in masks], axis=0)
        scores.append(
            lax.dot_general(k, spread, (((1,), (1,)), ((), ())), preferred_element_type=F32)
        )
    probabilities = []
    for s in scores:
        e = jnp.exp(s - jnp.max(s, axis=0, keepdims=True))
        probabilities.append((e * (1.0 / jnp.sum(e, axis=0, keepdims=True))).astype(BF))
    for (rows, g), p in zip(units, probabilities):
        v = packed[rows, 2 * D + g * 256 : 2 * D + (g + 1) * 256]
        for u in range(2):
            half = slice(u * 128, (u + 1) * 128)
            o = lax.dot_general(
                p[:, half], v[:, half], (((0,), (0,)), ((), ())), preferred_element_type=F32
            )
            start = g * 256 + u * 128
            attended[rows, start : start + 128] = jnp.where(low, o[:64], o[64:]).astype(BF)


def weight_copies(b, wqkv_hbm, wproj_hbm, wqkv, wproj, sems, psem):
    def piece(n):
        cols = pl.ds(pl.multiple_of(n * NC, NC), NC)
        return pltpu.make_async_copy(wqkv_hbm.at[b, :, cols], wqkv.at[:, cols], sems.at[n])

    return piece, pltpu.make_async_copy(wproj_hbm.at[b], wproj, psem)


def project_and_attend(pieces, piece, last, wqkv, normed, packed, attended):
    width = 3 * D // pieces

    @pl.loop(0, pieces)
    def _(n):
        for part in range(3 // pieces):
            piece(n * (3 // pieces) + part).wait()
        cols = pl.ds(pl.multiple_of(n * width, width), width)
        packed[:, cols] = jnp.dot(
            normed[...], wqkv[:, cols], preferred_element_type=F32
        ).astype(BF)

    @pl.loop(0, 2)
    def _(w):
        attend_windows(w * 8, 8, packed, attended)

    last.wait()


def local_kernel(
    b, x_hbm, gain_hbm, shift_hbm, wqkv_hbm, wproj_hbm, bias_hbm, out_ref, edge_ref,
    x_ref, gain, shift, bias, xsems, vsems, wqkv, wproj, normed, packed, attended, sems, psem,
):
    piece, last = weight_copies(b, wqkv_hbm, wproj_hbm, wqkv, wproj, sems, psem)
    vectors = [
        pltpu.make_async_copy(source, target, vsems.at[n])
        for n, (source, target) in enumerate(
            [(gain_hbm, gain), (shift_hbm, shift), (bias_hbm, bias)]
        )
    ]

    def tile(t):
        high = pl.ds(t // 4 * 8, 8)
        wide = pl.ds(pl.multiple_of(t % 4 * 16, 16), 16)
        return pltpu.make_async_copy(x_hbm.at[high, wide], x_ref.at[high, wide], xsems.at[t])

    for copy in vectors:
        copy.start()
    for t in range(8):
        tile(t).start()
    for copy in vectors:
        copy.wait()

    def norm(t):
        tile(t).wait()
        x = x_ref[pl.ds(t // 4 * 8, 8), pl.ds(pl.multiple_of(t % 4 * 16, 16), 16), :]
        x = x.astype(F32).reshape(8, 2, 8, D)
        for s in range(2):
            normed[pl.ds(pl.multiple_of(t * 128 + s * 64, 64), 64), :] = normalise(
                x[:, s].reshape(64, D), gain[b : b + 1], shift[b : b + 1]
            )

    pl.loop(0, 2, unroll=2)(norm)
    piece(0).start()
    pl.loop(2, 6, unroll=4)(norm)
    for n in range(1, 3 * D // NC):
        piece(n).start()
    last.start()
    pl.loop(6, 8, unroll=2)(norm)

    project_and_attend(3, piece, last, wqkv, normed, packed, attended)

    @pl.loop(0, D // NC)
    def _(n):
        cols = pl.ds(pl.multiple_of(n * NC, NC), NC)
        update = jnp.dot(attended[...], wproj[:, cols], preferred_element_type=F32)
        update = update + bias[b : b + 1, cols]
        for t in range(8):
            high, wide = slice(t // 4 * 8, t // 4 * 8 + 8), slice(t % 4 * 16, t % 4 * 16 + 16)
            x = x_ref[high, wide, cols].astype(F32).reshape(8, 2, 8, NC)
            for s in range(2):
                for r in range(8):
                    at = t * 128 + s * 64 + r * 8
                    tile = update[at : at + 8] + x[r, s]
                    for c in range(CHUNKS):
                        start = (t % 4 * 16 + s * 8) * PITCH + (t // 4 * 8 + r) * CHUNKS + c
                        part = tile[:, c * LANES : (c + 1) * LANES]
                        out_ref[pl.ds(start, 8, stride=PITCH), :] = part

    for side in range(2):
        start = (COLS - 2 + side) * PITCH
        column = out_ref[start : start + ROWS * CHUNKS, :]
        edge_ref[side * ROWS * CHUNKS : (side + 1) * ROWS * CHUNKS, :] = column.astype(BF)


ATTENTION_SCRATCH = [
    pltpu.VMEM((D, 3 * D), BF),
    pltpu.VMEM((D, D), BF),
    pltpu.VMEM((T, D), BF),
    pltpu.VMEM((T, 3 * D), BF),
    pltpu.VMEM((T, D), BF),
    pltpu.SemaphoreType.DMA((3 * D // NC,)),
    pltpu.SemaphoreType.DMA,
]


def local_attention(b, x, gain, shift, wqkv, wproj, bias):
    edge = jax.ShapeDtypeStruct((2 * ROWS * CHUNKS, LANES), BF)
    x, gain, shift, wqkv, wproj, bias = [
        pltpu.with_memory_space_constraint(a, pltpu.HBM)
        for a in (x, gain, shift, wqkv, wproj, bias)
    ]
    return pl.pallas_call(
        functools.partial(local_kernel, b),
        out_shape=(jax.ShapeDtypeStruct((COLS * PITCH, LANES), F32), edge),
        in_specs=[ANY] * 6,
        out_specs=(VM, VM),
        scratch_shapes=[
            pltpu.VMEM((ROWS, COLS, D), BF),
            pltpu.VMEM((2, D), F32),
            pltpu.VMEM((2, D), F32),
            pltpu.VMEM((2, D), F32),
            pltpu.SemaphoreType.DMA((8,)),
            pltpu.SemaphoreType.DMA((3,)),
        ]
        + ATTENTION_SCRATCH,
        compiler_params=pltpu.CompilerParams(vmem_limit_bytes=40 * 2**20),
        name="local_attention",
    )(x, gain, shift, wqkv, wproj, bias)


def place(col, row, chunk):
    return pl.ds(col * STRIDE + row * CHUNKS + chunk, 8, stride=STRIDE)


def widen(flat, wide):
    @pl.loop(0, 16)
    def _(n):
        rows = pl.ds(pl.multiple_of(n * 576, 576), 576)
        wide[rows, :] = flat[rows, :].astype(F32)


def narrow(wide, flat):
    @pl.loop(0, 16)
    def _(n):
        rows = pl.ds(pl.multiple_of(n * 576, 576), 576)
        flat[rows, :] = wide[rows, :].astype(BF)


def shuffled_kernel(
    b, in_ref, gain, shift, wqkv_hbm, wproj_hbm, bias, out_ref,
    wide, stream, wqkv, wproj, normed, packed, attended, sems, psem,
):
    piece, last = weight_copies(b, wqkv_hbm, wproj_hbm, wqkv, wproj, sems, psem)
    for n in range(3 * D // NC):
        piece(n).start()
    last.start()
    widen(in_ref, wide)

    @pl.loop(0, CHUNKS)
    def _(c):
        for i in range(7):
            above, below = i * 8, (i + 1) * 8
            wide[place(below, 1, c), :] += wide[place(above, EXT - 1, c), :]
            wide[place(above, EXT - 2, c), :] += wide[place(below, 0, c), :]

    @pl.loop(0, 16, unroll=4)
    def _(p):
        x = jnp.concatenate(
            [
                jnp.concatenate([wide[place(i * 8, p + 1, c), :] for c in range(CHUNKS)], axis=1)
                for i in range(8)
            ],
            axis=0,
        ).astype(BF)
        rows = pl.ds(pl.multiple_of(p * 64, 64), 64)
        stream[rows, :] = x
        normed[rows, :] = normalise(x.astype(F32), gain[b : b + 1], shift[b : b + 1])

    project_and_attend(1, piece, last, wqkv, normed, packed, attended)

    @pl.loop(0, D // NC)
    def _(n):
        cols = pl.ds(pl.multiple_of(n * NC, NC), NC)
        update = jnp.dot(attended[...], wproj[:, cols], preferred_element_type=F32)
        update = update + bias[b : b + 1, cols] + stream[:, cols].astype(F32)
        for u in range(NC // LANES):
            c = n * (NC // LANES) + u
            wide[place(0, 0, c), :] = jnp.zeros((8, LANES), F32)
            wide[place(56, EXT - 1, c), :] = jnp.zeros((8, LANES), F32)
            for p in range(16):
                for i in range(8):
                    tile = update[p * 64 + i * 8 : p * 64 + i * 8 + 8, u * LANES : (u + 1) * LANES]
                    wide[place(i * 8, p + 1, c), :] = tile
                    if p == 15 and i < 7:
                        wide[place(i * 8 + 8, 0, c), :] = tile
                    if p == 0 and i > 0:
                        wide[place(i * 8 - 8, EXT - 1, c), :] = tile

    narrow(wide, out_ref)


def shuffled_attention(b, x, gain, shift, wqkv, wproj, bias):
    return pl.pallas_call(
        functools.partial(shuffled_kernel, b),
        out_shape=jax.ShapeDtypeStruct((COLS * STRIDE, LANES), BF),
        in_specs=[VM, VM, VM, ANY, ANY, VM],
        out_specs=VM,
        scratch_shapes=[pltpu.VMEM((COLS * STRIDE, LANES), F32), pltpu.VMEM((T, D), BF)]
        + ATTENTION_SCRATCH,
        compiler_params=pltpu.CompilerParams(vmem_limit_bytes=48 * 2**20),
        name="shuffled_attention",
    )(
        x,
        gain,
        shift,
        pltpu.with_memory_space_constraint(wqkv, pltpu.HBM),
        pltpu.with_memory_space_constraint(wproj, pltpu.HBM),
        bias,
    )


def stage_taps(taps_ref, bias_ref, b, tiles):
    for c in range(CHUNKS):
        lanes = slice(c * LANES, (c + 1) * LANES)
        for t in range(9):
            tap = taps_ref[b, t : t + 1, lanes]
            tiles[t * 8 + c : t * 8 + c + 1, :] = tap + 1.0 if t == 4 else tap
        tiles[72 + c : 73 + c, :] = bias_ref[b : b + 1, lanes]


def column_sums(load, rows, low, high, taps):
    loaded = {}
    sums = []
    for row in rows:
        total = None
        for step in range(3):
            source = row + step - 1
            if low <= source < high:
                for col in range(3):
                    if (source, col) not in loaded:
                        loaded[source, col] = load(source, col)
                    term = taps[3 * step + col] * loaded[source, col]
                    total = term if total is None else total + term
        sums.append(total)
    return sums


def position():
    return lax.axis_index("pairs") * 2 + lax.axis_index("core")


def spread_column(k, load, tiles, out_ref, scales=(None, None, None)):
    taps = []
    for t in range(9):
        tap = tiles[t * 8 : t * 8 + 8, :]
        taps.append(tap if scales[t % 3] is None else tap * scales[t % 3])
    bias = tiles[72:80, :]
    sums = column_sums(load, range(-1, ROWS + 1), 0, ROWS, taps)
    sums[1:-1] = [total + bias for total in sums[1:-1]]
    for pair in range(EXT // 2):
        rows = pl.ds(pl.multiple_of(k * STRIDE + pair * 16, 16), 16)
        both = jnp.concatenate(sums[2 * pair : 2 * pair + 2], axis=0)
        out_ref[rows, :] = both.astype(BF)


def inner_spread_kernel(b, x_ref, taps_ref, bias_ref, out_ref, tiles):
    stage_taps(taps_ref, bias_ref, b, tiles)

    @pl.loop(2, COLS, unroll=2)
    def _(k):
        def load(r, col):
            return x_ref[pl.ds(pl.multiple_of((k + col - 2) * PITCH + r * 8, 8), 8), :]

        spread_column(k, load, tiles, out_ref)


def outer_spread_kernel(
    b, x_ref, edge_ref, taps_ref, bias_ref, _, out_ref, edge, held, tiles, sem
):
    inner = jnp.where(position() == 0, 0.0, 1.0)
    stage_taps(taps_ref, bias_ref, b, tiles)
    edge[...] = edge_ref[...].astype(F32)
    for k, scales in enumerate([(None, None, inner), (inner, None, None)]):

        def load(r, col):
            if k + col < 2:
                start = ((k + col) * ROWS + r) * CHUNKS
                return edge[start : start + 8, :]
            start = (k + col - 2) * PITCH + r * 8
            return x_ref[start : start + 8, :]

        spread_column(k, load, tiles, held, scales)
    copy = pltpu.make_async_copy(held, out_ref.at[pl.ds(0, 2 * STRIDE)], sem)
    copy.start()
    copy.wait()


def spread_convolution(b, x, edge, taps, bias):
    out = jax.ShapeDtypeStruct((COLS * STRIDE, LANES), BF)
    params = pltpu.CompilerParams(vmem_limit_bytes=24 * 2**20)
    inner = pl.pallas_call(
        functools.partial(inner_spread_kernel, b),
        out_shape=out,
        in_specs=[VM] * 3,
        out_specs=VM,
        scratch_shapes=[pltpu.VMEM((80, LANES), F32)],
        compiler_params=params,
        cost_estimate=pl.CostEstimate(flops=10**9, bytes_accessed=10**7, transcendentals=0),
        name="inner_spread_convolution",
    )(x, taps, bias)
    return pl.pallas_call(
        functools.partial(outer_spread_kernel, b),
        out_shape=out,
        in_specs=[VM] * 4 + [ANY],
        out_specs=ANY,
        scratch_shapes=[
            pltpu.VMEM((2 * ROWS * CHUNKS, LANES), F32),
            pltpu.VMEM((2 * STRIDE, LANES), BF),
            pltpu.VMEM((80, LANES), F32),
            pltpu.SemaphoreType.DMA,
        ],
        input_output_aliases={4: 0},
        compiler_params=params,
        name="outer_spread_convolution",
    )(x, edge, taps, bias, inner)


FIRST = 48


def columns_out(source, out_ref, first, sem):
    return pltpu.make_async_copy(source, out_ref.at[:, pl.ds(first, 16)], sem)


def final_columns(n, b, wide, natural, tiles, target):
    @pl.loop(0, 16, unroll=4)
    def _(w):
        taps = [tiles[t * 8 : t * 8 + 8, :] for t in range(9)]
        bias = tiles[72:80, :]

        def load(r, col):
            start = (n * 16 + w + col) * STRIDE + r * 8
            return wide[pl.ds(pl.multiple_of(start, 8), 8), :]

        sums = column_sums(load, range(1, EXT - 1), 0, EXT, taps)
        for row in range(ROWS):
            start = row * 128 + w // 8 * 64 + w % 8
            natural[pl.ds(start, 8, stride=8), :] = sums[row] + bias

    for row in range(ROWS):
        for c in range(CHUNKS):
            start = row * 128 + c * 8
            both = jnp.concatenate(
                [natural[start : start + 8, :], natural[start + 64 : start + 72, :]], axis=0
            )
            target[row, :, c * LANES : (c + 1) * LANES] = both.astype(BF)


def first_final_kernel(
    b, in_ref, taps_ref, bias_ref, out_ref, tail_ref, wide, natural, held, tiles, sems
):
    inner = jnp.where(position() == 0, 0.0, 1.0)
    stage_taps(taps_ref, bias_ref, b, tiles)

    @pl.loop(0, (FIRST + 2) // 2)
    def _(n):
        rows = pl.ds(pl.multiple_of(n * 2 * STRIDE, 2 * STRIDE), 2 * STRIDE)
        wide[rows, :] = in_ref[rows, :].astype(F32)

    wide[:STRIDE, :] = wide[:STRIDE, :] * inner
    count = FIRST // 16 - 1
    copies = [columns_out(held.at[n], out_ref, n * 16, sems.at[n]) for n in range(count)]
    for n in range(count):
        final_columns(n, b, wide, natural, tiles, held.at[n])
        copies[n].start()
    final_columns(count, b, wide, natural, tiles, tail_ref)
    for copy in copies:
        copy.wait()


def second_final_kernel(
    b, in_ref, edge_ref, taps_ref, bias_ref, tail_ref, _, out_ref,
    wide, natural, held, tiles, sems,
):
    outer = jnp.where(position() == 15, 0.0, 1.0)
    tail = columns_out(tail_ref, out_ref, FIRST - 16, sems.at[0])
    tail.start()
    stage_taps(taps_ref, bias_ref, b, tiles)
    count = (COLS - FIRST) * STRIDE
    wide[:count, :] = in_ref[FIRST * STRIDE :, :].astype(F32)
    wide[count : count + STRIDE, :] = edge_ref[:STRIDE, :].astype(F32)
    wide[count + STRIDE :, :] = edge_ref[STRIDE:, :].astype(F32) * outer
    final_columns(0, b, wide, natural, tiles, held)
    own = columns_out(held, out_ref, FIRST, sems.at[1])
    own.start()
    tail.wait()
    own.wait()


def final_convolution(b, x, edge, taps, bias):
    out = jax.ShapeDtypeStruct((ROWS, COLS, D), BF)
    block = (ROWS, 16, D)
    params = pltpu.CompilerParams(vmem_limit_bytes=24 * 2**20)
    first, tail = pl.pallas_call(
        functools.partial(first_final_kernel, b),
        out_shape=(out, jax.ShapeDtypeStruct(block, BF)),
        in_specs=[VM] * 3,
        out_specs=(ANY, VM),
        scratch_shapes=[
            pltpu.VMEM(((FIRST + 2) * STRIDE, LANES), F32),
            pltpu.VMEM((ROWS * 128, LANES), F32),
            pltpu.VMEM((FIRST // 16 - 1,) + block, BF),
            pltpu.VMEM((80, LANES), F32),
            pltpu.SemaphoreType.DMA((FIRST // 16 - 1,)),
        ],
        compiler_params=params,
        cost_estimate=pl.CostEstimate(flops=10**9, bytes_accessed=10**7, transcendentals=0),
        name="first_final_convolution",
    )(x, taps, bias)
    return pl.pallas_call(
        functools.partial(second_final_kernel, b),
        out_shape=out,
        in_specs=[VM] * 5 + [ANY],
        out_specs=ANY,
        scratch_shapes=[
            pltpu.VMEM(((COLS - FIRST + 2) * STRIDE, LANES), F32),
            pltpu.VMEM((ROWS * 128, LANES), F32),
            pltpu.VMEM(block, BF),
            pltpu.VMEM((80, LANES), F32),
            pltpu.SemaphoreType.DMA((2,)),
        ],
        input_output_aliases={5: 0},
        compiler_params=params,
        name="second_final_convolution",
    )(x, edge, taps, bias, tail, first)


def shifted(columns, step):
    axes = ("pairs", "core")
    count = lax.axis_size(axes)
    return lax.ppermute(columns, axes, [(i, (i + step) % count) for i in range(count)])


def exchange(flat):
    blocks = flat.reshape(COLS, STRIDE, LANES)
    return lax.all_to_all(blocks, ("rows", "pairs"), split_axis=0, concat_axis=0, tiled=True)


def body(patches, gain, shift, wqkv, wproj, bias, taps, conv_bias):
    block_one, edge = local_attention(0, patches, gain, shift, wqkv, wproj, bias)
    outgoing = spread_convolution(0, block_one, shifted(edge, 1), taps, conv_bias)
    arrived = exchange(outgoing).reshape(COLS * STRIDE, LANES)
    returning = shuffled_attention(1, arrived, gain, shift, wqkv, wproj, bias)
    restored = exchange(returning).reshape(COLS * STRIDE, LANES)
    edge = shifted(restored[: 2 * STRIDE], -1)
    return final_convolution(1, restored, edge, taps, conv_bias)


def solution(mesh):
    grid = Mesh(mesh.devices.reshape(8, 8, 2), ("rows", "pairs", "core"))
    split = P("rows", ("pairs", "core"), None)
    return jax.shard_map(
        body,
        mesh=grid,
        in_specs=(split, P(), P(), P(), P(), P(), P(), P()),
        out_specs=split,
        check_vma=False,
    )
```

```python
import functools

import jax
import jax.numpy as jnp
from jax import lax
from jax.experimental import pallas as pl
from jax.experimental.pallas import tpu as pltpu
from jax.sharding import Mesh
from jax.sharding import PartitionSpec as P

BF = jnp.bfloat16
F32 = jnp.float32
D = 1024
T = 1024
NC = 1024
ROWS, COLS = 16, 64
EXT = ROWS + 2
LANES = 128
CHUNKS = D // LANES
STRIDE = EXT * CHUNKS
PITCH = (ROWS + 1) * CHUNKS

VM = pl.BlockSpec(memory_space=pltpu.VMEM)
ANY = pl.BlockSpec(memory_space=pl.ANY)


def normalise(x, gain, shift):
    center = x - jnp.mean(x, axis=-1, keepdims=True)
    spread = jnp.mean(center * center, axis=-1, keepdims=True)
    return (center * lax.rsqrt(spread + 1e-05) * gain + shift).astype(BF)


def attend_windows(first, count, packed, attended):
    lane = lax.broadcasted_iota(jnp.int32, (64, 128), 1) // 64
    masks = [jnp.where(lane == h, 0.125, 0.0).astype(BF) for h in range(2)]
    blank = jnp.zeros((128, 128), BF)
    low = lax.broadcasted_iota(jnp.int32, (64, 128), 1) < 64
    units = [
        (pl.ds(pl.multiple_of((first + i) * 64, 64), 64), g)
        for i in range(count)
        for g in range(4)
    ]
    scores = []
    for rows, g in units:
        q = packed[rows, g * 256 : (g + 1) * 256]
        k = packed[rows, D + g * 256 : D + (g + 1) * 256]
        one, two = [
            jnp.concatenate([q[:, u : u + 128] * mask for mask in masks], axis=0) for u in (0, 128)
        ]
        spread = jnp.concatenate(
            [
                jnp.concatenate([one, blank], axis=1),
                jnp.concatenate([blank, two], axis=1),
            ],
            axis=0,
        )
        scores.append(
            lax.dot_general(k, spread, (((1,), (1,)), ((), ())), preferred_element_type=F32)
        )
    probabilities = []
    for s in scores:
        e = jnp.exp(s - jnp.max(s, axis=0, keepdims=True))
        probabilities.append((e * (1.0 / jnp.sum(e, axis=0, keepdims=True))).astype(BF))
    for (rows, g), p in zip(units, probabilities):
        v = packed[rows, 2 * D + g * 256 : 2 * D + (g + 1) * 256]
        for u in range(2):
            half = slice(u * 128, (u + 1) * 128)
            o = lax.dot_general(
                p[:, half], v[:, half], (((0,), (0,)), ((), ())), preferred_element_type=F32
            )
            start = g * 256 + u * 128
            attended[rows, start : start + 128] = jnp.where(low, o[:64], o[64:]).astype(BF)


def weight_copies(b, wqkv_hbm, wproj_hbm, wqkv, wproj, sems, psem):
    def piece(n):
        cols = pl.ds(pl.multiple_of(n * NC, NC), NC)
        return pltpu.make_async_copy(wqkv_hbm.at[b, :, cols], wqkv.at[:, cols], sems.at[n])

    return piece, pltpu.make_async_copy(wproj_hbm.at[b], wproj, psem)


def project_and_attend(pieces, piece, last, wqkv, normed, packed, attended):
    width = 3 * D // pieces

    @pl.loop(0, pieces)
    def _(n):
        for part in range(3 // pieces):
            piece(n * (3 // pieces) + part).wait()
        cols = pl.ds(pl.multiple_of(n * width, width), width)
        packed[:, cols] = jnp.dot(
            normed[...], wqkv[:, cols], preferred_element_type=F32
        ).astype(BF)

    @pl.loop(0, 2)
    def _(w):
        attend_windows(w * 8, 8, packed, attended)

    last.wait()


def local_kernel(
    b, x_hbm, gain_hbm, shift_hbm, wqkv_hbm, wproj_hbm, bias_hbm, out_ref, edge_ref,
    x_ref, gain, shift, bias, xsems, vsems, wqkv, wproj, normed, packed, attended, sems, psem,
):
    piece, last = weight_copies(b, wqkv_hbm, wproj_hbm, wqkv, wproj, sems, psem)
    vectors = [
        pltpu.make_async_copy(source, target, vsems.at[n])
        for n, (source, target) in enumerate(
            [(gain_hbm, gain), (shift_hbm, shift), (bias_hbm, bias)]
        )
    ]

    def tile(t):
        high = pl.ds(t // 4 * 8, 8)
        wide = pl.ds(pl.multiple_of(t % 4 * 16, 16), 16)
        return pltpu.make_async_copy(x_hbm.at[high, wide], x_ref.at[high, wide], xsems.at[t])

    for copy in vectors:
        copy.start()
    for t in range(8):
        tile(t).start()
    for copy in vectors:
        copy.wait()

    def norm(t):
        tile(t).wait()
        x = x_ref[pl.ds(t // 4 * 8, 8), pl.ds(pl.multiple_of(t % 4 * 16, 16), 16), :]
        x = x.astype(F32).reshape(8, 2, 8, D)
        for s in range(2):
            normed[pl.ds(pl.multiple_of(t * 128 + s * 64, 64), 64), :] = normalise(
                x[:, s].reshape(64, D), gain[b : b + 1], shift[b : b + 1]
            )

    pl.loop(0, 2, unroll=2)(norm)
    piece(0).start()
    pl.loop(2, 6, unroll=4)(norm)
    for n in range(1, 3 * D // NC):
        piece(n).start()
    last.start()
    pl.loop(6, 8, unroll=2)(norm)

    project_and_attend(3, piece, last, wqkv, normed, packed, attended)

    @pl.loop(0, D // NC)
    def _(n):
        cols = pl.ds(pl.multiple_of(n * NC, NC), NC)
        update = jnp.dot(attended[...], wproj[:, cols], preferred_element_type=F32)
        update = update + bias[b : b + 1, cols]
        for t in range(8):
            high, wide = slice(t // 4 * 8, t // 4 * 8 + 8), slice(t % 4 * 16, t % 4 * 16 + 16)
            x = x_ref[high, wide, cols].astype(F32).reshape(8, 2, 8, NC)
            for s in range(2):
                for r in range(8):
                    at = t * 128 + s * 64 + r * 8
                    tile = update[at : at + 8] + x[r, s]
                    for c in range(CHUNKS):
                        start = (t % 4 * 16 + s * 8) * PITCH + (t // 4 * 8 + r) * CHUNKS + c
                        part = tile[:, c * LANES : (c + 1) * LANES]
                        out_ref[pl.ds(start, 8, stride=PITCH), :] = part

    for side in range(2):
        start = (COLS - 2 + side) * PITCH
        column = out_ref[start : start + ROWS * CHUNKS, :]
        edge_ref[side * ROWS * CHUNKS : (side + 1) * ROWS * CHUNKS, :] = column.astype(BF)


ATTENTION_SCRATCH = [
    pltpu.VMEM((D, 3 * D), BF),
    pltpu.VMEM((D, D), BF),
    pltpu.VMEM((T, D), BF),
    pltpu.VMEM((T, 3 * D), BF),
    pltpu.VMEM((T, D), BF),
    pltpu.SemaphoreType.DMA((3 * D // NC,)),
    pltpu.SemaphoreType.DMA,
]


def local_attention(b, x, gain, shift, wqkv, wproj, bias):
    edge = jax.ShapeDtypeStruct((2 * ROWS * CHUNKS, LANES), BF)
    x, gain, shift, wqkv, wproj, bias = [
        pltpu.with_memory_space_constraint(a, pltpu.HBM)
        for a in (x, gain, shift, wqkv, wproj, bias)
    ]
    return pl.pallas_call(
        functools.partial(local_kernel, b),
        out_shape=(jax.ShapeDtypeStruct((COLS * PITCH, LANES), F32), edge),
        in_specs=[ANY] * 6,
        out_specs=(VM, VM),
        scratch_shapes=[
            pltpu.VMEM((ROWS, COLS, D), BF),
            pltpu.VMEM((2, D), F32),
            pltpu.VMEM((2, D), F32),
            pltpu.VMEM((2, D), F32),
            pltpu.SemaphoreType.DMA((8,)),
            pltpu.SemaphoreType.DMA((3,)),
        ]
        + ATTENTION_SCRATCH,
        compiler_params=pltpu.CompilerParams(vmem_limit_bytes=40 * 2**20),
        name="local_attention",
    )(x, gain, shift, wqkv, wproj, bias)


def place(col, row, chunk):
    return pl.ds(col * STRIDE + row * CHUNKS + chunk, 8, stride=STRIDE)


def widen(flat, wide):
    @pl.loop(0, 8)
    def _(n):
        rows = pl.ds(pl.multiple_of(n * 1152, 1152), 1152)
        wide[rows, :] = flat[rows, :].astype(F32)


def narrow(wide, flat):
    @pl.loop(0, 8)
    def _(n):
        rows = pl.ds(pl.multiple_of(n * 1152, 1152), 1152)
        flat[rows, :] = wide[rows, :].astype(BF)


def shuffled_kernel(
    b, in_ref, gain, shift, wqkv_hbm, wproj_hbm, bias, out_ref,
    wide, stream, wqkv, wproj, normed, packed, attended, sems, psem,
):
    piece, last = weight_copies(b, wqkv_hbm, wproj_hbm, wqkv, wproj, sems, psem)
    for n in range(3 * D // NC):
        piece(n).start()
    last.start()
    widen(in_ref, wide)

    @pl.loop(0, CHUNKS)
    def _(c):
        for i in range(7):
            above, below = i * 8, (i + 1) * 8
            wide[place(below, 1, c), :] += wide[place(above, EXT - 1, c), :]
            wide[place(above, EXT - 2, c), :] += wide[place(below, 0, c), :]

    @pl.loop(0, 16, unroll=8)
    def _(p):
        x = jnp.concatenate(
            [
                jnp.concatenate([wide[place(i * 8, p + 1, c), :] for c in range(CHUNKS)], axis=1)
                for i in range(8)
            ],
            axis=0,
        ).astype(BF)
        rows = pl.ds(pl.multiple_of(p * 64, 64), 64)
        stream[rows, :] = x
        normed[rows, :] = normalise(x.astype(F32), gain[b : b + 1], shift[b : b + 1])

    project_and_attend(1, piece, last, wqkv, normed, packed, attended)

    @pl.loop(0, D // NC)
    def _(n):
        cols = pl.ds(pl.multiple_of(n * NC, NC), NC)
        update = jnp.dot(attended[...], wproj[:, cols], preferred_element_type=F32)
        update = update + bias[b : b + 1, cols] + stream[:, cols].astype(F32)
        for u in range(NC // LANES):
            c = n * (NC // LANES) + u
            wide[place(0, 0, c), :] = jnp.zeros((8, LANES), F32)
            wide[place(56, EXT - 1, c), :] = jnp.zeros((8, LANES), F32)
            for p in range(16):
                for i in range(8):
                    tile = update[p * 64 + i * 8 : p * 64 + i * 8 + 8, u * LANES : (u + 1) * LANES]
                    wide[place(i * 8, p + 1, c), :] = tile
                    if p == 15 and i < 7:
                        wide[place(i * 8 + 8, 0, c), :] = tile
                    if p == 0 and i > 0:
                        wide[place(i * 8 - 8, EXT - 1, c), :] = tile

    narrow(wide, out_ref)


def shuffled_attention(b, x, gain, shift, wqkv, wproj, bias):
    return pl.pallas_call(
        functools.partial(shuffled_kernel, b),
        out_shape=jax.ShapeDtypeStruct((COLS * STRIDE, LANES), BF),
        in_specs=[VM, VM, VM, ANY, ANY, VM],
        out_specs=VM,
        scratch_shapes=[pltpu.VMEM((COLS * STRIDE, LANES), F32), pltpu.VMEM((T, D), BF)]
        + ATTENTION_SCRATCH,
        compiler_params=pltpu.CompilerParams(vmem_limit_bytes=48 * 2**20),
        name="shuffled_attention",
    )(
        x,
        gain,
        shift,
        pltpu.with_memory_space_constraint(wqkv, pltpu.HBM),
        pltpu.with_memory_space_constraint(wproj, pltpu.HBM),
        bias,
    )


def stage_taps(taps_ref, bias_ref, b, tiles):
    for c in range(CHUNKS):
        lanes = slice(c * LANES, (c + 1) * LANES)
        for t in range(9):
            tap = taps_ref[b, t : t + 1, lanes]
            tiles[t * 8 + c : t * 8 + c + 1, :] = tap + 1.0 if t == 4 else tap
        tiles[72 + c : 73 + c, :] = bias_ref[b : b + 1, lanes]


def column_sums(load, rows, low, high, taps):
    loaded = {}
    sums = []
    for row in rows:
        total = None
        for step in range(3):
            source = row + step - 1
            if low <= source < high:
                for col in range(3):
                    if (source, col) not in loaded:
                        loaded[source, col] = load(source, col)
                    term = taps[3 * step + col] * loaded[source, col]
                    total = term if total is None else total + term
        sums.append(total)
    return sums


def position():
    return lax.axis_index("pairs") * 2 + lax.axis_index("core")


def spread_column(k, load, tiles, out_ref, scales=(None, None, None)):
    taps = []
    for t in range(9):
        tap = tiles[t * 8 : t * 8 + 8, :]
        taps.append(tap if scales[t % 3] is None else tap * scales[t % 3])
    bias = tiles[72:80, :]
    sums = column_sums(load, range(-1, ROWS + 1), 0, ROWS, taps)
    sums[1:-1] = [total + bias for total in sums[1:-1]]
    for pair in range(EXT // 2):
        rows = pl.ds(pl.multiple_of(k * STRIDE + pair * 16, 16), 16)
        both = jnp.concatenate(sums[2 * pair : 2 * pair + 2], axis=0)
        out_ref[rows, :] = both.astype(BF)


def inner_spread_kernel(b, x_ref, taps_ref, bias_ref, out_ref, tiles):
    stage_taps(taps_ref, bias_ref, b, tiles)

    @pl.loop(2, COLS, unroll=2)
    def _(k):
        def load(r, col):
            return x_ref[pl.ds(pl.multiple_of((k + col - 2) * PITCH + r * 8, 8), 8), :]

        spread_column(k, load, tiles, out_ref)


def outer_spread_kernel(
    b, x_ref, edge_ref, taps_ref, bias_ref, _, out_ref, edge, held, tiles, sem
):
    inner = jnp.where(position() == 0, 0.0, 1.0)
    stage_taps(taps_ref, bias_ref, b, tiles)
    edge[...] = edge_ref[...].astype(F32)
    for k, scales in enumerate([(None, None, inner), (inner, None, None)]):

        def load(r, col):
            if k + col < 2:
                start = ((k + col) * ROWS + r) * CHUNKS
                return edge[start : start + 8, :]
            start = (k + col - 2) * PITCH + r * 8
            return x_ref[start : start + 8, :]

        spread_column(k, load, tiles, held, scales)
    copy = pltpu.make_async_copy(held, out_ref.at[pl.ds(0, 2 * STRIDE)], sem)
    copy.start()
    copy.wait()


def spread_convolution(b, x, edge, taps, bias):
    out = jax.ShapeDtypeStruct((COLS * STRIDE, LANES), BF)
    params = pltpu.CompilerParams(vmem_limit_bytes=24 * 2**20)
    inner = pl.pallas_call(
        functools.partial(inner_spread_kernel, b),
        out_shape=out,
        in_specs=[VM] * 3,
        out_specs=VM,
        scratch_shapes=[pltpu.VMEM((80, LANES), F32)],
        compiler_params=params,
        cost_estimate=pl.CostEstimate(flops=10**9, bytes_accessed=10**7, transcendentals=0),
        name="inner_spread_convolution",
    )(x, taps, bias)
    return pl.pallas_call(
        functools.partial(outer_spread_kernel, b),
        out_shape=out,
        in_specs=[VM] * 4 + [ANY],
        out_specs=ANY,
        scratch_shapes=[
            pltpu.VMEM((2 * ROWS * CHUNKS, LANES), F32),
            pltpu.VMEM((2 * STRIDE, LANES), BF),
            pltpu.VMEM((80, LANES), F32),
            pltpu.SemaphoreType.DMA,
        ],
        input_output_aliases={4: 0},
        compiler_params=params,
        name="outer_spread_convolution",
    )(x, edge, taps, bias, inner)


FIRST = 48


def columns_out(source, out_ref, first, sem):
    return pltpu.make_async_copy(source, out_ref.at[:, pl.ds(first, 16)], sem)


def final_columns(n, b, wide, natural, tiles, target):
    @pl.loop(0, 16, unroll=4)
    def _(w):
        taps = [tiles[t * 8 : t * 8 + 8, :] for t in range(9)]
        bias = tiles[72:80, :]

        def load(r, col):
            start = (n * 16 + w + col) * STRIDE + r * 8
            return wide[pl.ds(pl.multiple_of(start, 8), 8), :]

        sums = column_sums(load, range(1, EXT - 1), 0, EXT, taps)
        for row in range(ROWS):
            start = row * 128 + w // 8 * 64 + w % 8
            natural[pl.ds(start, 8, stride=8), :] = sums[row] + bias

    for row in range(ROWS):
        for c in range(CHUNKS):
            start = row * 128 + c * 8
            both = jnp.concatenate(
                [natural[start : start + 8, :], natural[start + 64 : start + 72, :]], axis=0
            )
            target[row, :, c * LANES : (c + 1) * LANES] = both.astype(BF)


def first_final_kernel(
    b, in_ref, taps_ref, bias_ref, out_ref, tail_ref, wide, natural, held, tiles, sems
):
    inner = jnp.where(position() == 0, 0.0, 1.0)
    stage_taps(taps_ref, bias_ref, b, tiles)

    @pl.loop(0, (FIRST + 2) // 2)
    def _(n):
        rows = pl.ds(pl.multiple_of(n * 2 * STRIDE, 2 * STRIDE), 2 * STRIDE)
        wide[rows, :] = in_ref[rows, :].astype(F32)

    wide[:STRIDE, :] = wide[:STRIDE, :] * inner
    count = FIRST // 16 - 1
    copies = [columns_out(held.at[n], out_ref, n * 16, sems.at[n]) for n in range(count)]
    for n in range(count):
        final_columns(n, b, wide, natural, tiles, held.at[n])
        copies[n].start()
    final_columns(count, b, wide, natural, tiles, tail_ref)
    for copy in copies:
        copy.wait()


def second_final_kernel(
    b, in_ref, edge_ref, taps_ref, bias_ref, tail_ref, _, out_ref,
    wide, natural, held, tiles, sems,
):
    outer = jnp.where(position() == 15, 0.0, 1.0)
    tail = columns_out(tail_ref, out_ref, FIRST - 16, sems.at[0])
    tail.start()
    stage_taps(taps_ref, bias_ref, b, tiles)
    count = (COLS - FIRST) * STRIDE
    wide[:count, :] = in_ref[FIRST * STRIDE :, :].astype(F32)
    wide[count : count + STRIDE, :] = edge_ref[:STRIDE, :].astype(F32)
    wide[count + STRIDE :, :] = edge_ref[STRIDE:, :].astype(F32) * outer
    final_columns(0, b, wide, natural, tiles, held)
    own = columns_out(held, out_ref, FIRST, sems.at[1])
    own.start()
    tail.wait()
    own.wait()


def final_convolution(b, x, edge, taps, bias):
    out = jax.ShapeDtypeStruct((ROWS, COLS, D), BF)
    block = (ROWS, 16, D)
    params = pltpu.CompilerParams(vmem_limit_bytes=24 * 2**20)
    first, tail = pl.pallas_call(
        functools.partial(first_final_kernel, b),
        out_shape=(out, jax.ShapeDtypeStruct(block, BF)),
        in_specs=[VM] * 3,
        out_specs=(ANY, VM),
        scratch_shapes=[
            pltpu.VMEM(((FIRST + 2) * STRIDE, LANES), F32),
            pltpu.VMEM((ROWS * 128, LANES), F32),
            pltpu.VMEM((FIRST // 16 - 1,) + block, BF),
            pltpu.VMEM((80, LANES), F32),
            pltpu.SemaphoreType.DMA((FIRST // 16 - 1,)),
        ],
        compiler_params=params,
        cost_estimate=pl.CostEstimate(flops=10**9, bytes_accessed=10**7, transcendentals=0),
        name="first_final_convolution",
    )(x, taps, bias)
    return pl.pallas_call(
        functools.partial(second_final_kernel, b),
        out_shape=out,
        in_specs=[VM] * 5 + [ANY],
        out_specs=ANY,
        scratch_shapes=[
            pltpu.VMEM(((COLS - FIRST + 2) * STRIDE, LANES), F32),
            pltpu.VMEM((ROWS * 128, LANES), F32),
            pltpu.VMEM(block, BF),
            pltpu.VMEM((80, LANES), F32),
            pltpu.SemaphoreType.DMA((2,)),
        ],
        input_output_aliases={5: 0},
        compiler_params=params,
        name="second_final_convolution",
    )(x, edge, taps, bias, tail, first)


def shifted(columns, step):
    axes = ("pairs", "core")
    count = lax.axis_size(axes)
    return lax.ppermute(columns, axes, [(i, (i + step) % count) for i in range(count)])


def exchange(flat):
    blocks = flat.reshape(COLS, STRIDE, LANES)
    return lax.all_to_all(blocks, ("rows", "pairs"), split_axis=0, concat_axis=0, tiled=True)


def body(patches, gain, shift, wqkv, wproj, bias, taps, conv_bias):
    block_one, edge = local_attention(0, patches, gain, shift, wqkv, wproj, bias)
    outgoing = spread_convolution(0, block_one, shifted(edge, 1), taps, conv_bias)
    arrived = exchange(outgoing).reshape(COLS * STRIDE, LANES)
    returning = shuffled_attention(1, arrived, gain, shift, wqkv, wproj, bias)
    restored = exchange(returning).reshape(COLS * STRIDE, LANES)
    edge = shifted(restored[: 2 * STRIDE], -1)
    return final_convolution(1, restored, edge, taps, conv_bias)


def solution(mesh):
    grid = Mesh(mesh.devices.reshape(8, 8, 2), ("rows", "pairs", "core"))
    split = P("rows", ("pairs", "core"), None)
    return jax.shard_map(
        body,
        mesh=grid,
        in_specs=(split, P(), P(), P(), P(), P(), P(), P()),
        out_specs=split,
        check_vma=False,
    )
```

```python
import functools

import jax
import jax.numpy as jnp
from jax import lax
from jax.experimental import pallas as pl
from jax.experimental.pallas import tpu as pltpu
from jax.sharding import Mesh
from jax.sharding import PartitionSpec as P

BF = jnp.bfloat16
F32 = jnp.float32
D = 1024
T = 1024
NC = 1024
ROWS, COLS = 16, 64
EXT = ROWS + 2
LANES = 128
CHUNKS = D // LANES
STRIDE = EXT * CHUNKS
PITCH = (ROWS + 1) * CHUNKS

VM = pl.BlockSpec(memory_space=pltpu.VMEM)
ANY = pl.BlockSpec(memory_space=pl.ANY)


def normalise(x, gain, shift):
    center = x - jnp.mean(x, axis=-1, keepdims=True)
    spread = jnp.mean(center * center, axis=-1, keepdims=True)
    return (center * lax.rsqrt(spread + 1e-05) * gain + shift).astype(BF)


def attend_windows(first, count, packed, attended):
    lane = lax.broadcasted_iota(jnp.int32, (64, 128), 1) // 64
    masks = [jnp.where(lane == h, 0.125, 0.0).astype(BF) for h in range(2)]
    blank = jnp.zeros((128, 128), BF)
    low = lax.broadcasted_iota(jnp.int32, (64, 128), 1) < 64
    units = [
        (pl.ds(pl.multiple_of((first + i) * 64, 64), 64), g)
        for i in range(count)
        for g in range(4)
    ]
    scores = []
    for rows, g in units:
        q = packed[rows, g * 256 : (g + 1) * 256]
        k = packed[rows, D + g * 256 : D + (g + 1) * 256]
        one, two = [
            jnp.concatenate([q[:, u : u + 128] * mask for mask in masks], axis=0) for u in (0, 128)
        ]
        spread = jnp.concatenate(
            [
                jnp.concatenate([one, blank], axis=1),
                jnp.concatenate([blank, two], axis=1),
            ],
            axis=0,
        )
        scores.append(
            lax.dot_general(k, spread, (((1,), (1,)), ((), ())), preferred_element_type=F32)
        )
    probabilities = []
    for s in scores:
        e = jnp.exp(s - jnp.max(s, axis=0, keepdims=True))
        probabilities.append((e * (1.0 / jnp.sum(e, axis=0, keepdims=True))).astype(BF))
    for (rows, g), p in zip(units, probabilities):
        v = packed[rows, 2 * D + g * 256 : 2 * D + (g + 1) * 256]
        for u in range(2):
            half = slice(u * 128, (u + 1) * 128)
            o = lax.dot_general(
                p[:, half], v[:, half], (((0,), (0,)), ((), ())), preferred_element_type=F32
            )
            start = g * 256 + u * 128
            attended[rows, start : start + 128] = jnp.where(low, o[:64], o[64:]).astype(BF)


def weight_copies(b, wqkv_hbm, wproj_hbm, wqkv, wproj, sems, psem):
    def piece(n):
        cols = pl.ds(pl.multiple_of(n * NC, NC), NC)
        return pltpu.make_async_copy(wqkv_hbm.at[b, :, cols], wqkv.at[:, cols], sems.at[n])

    return piece, pltpu.make_async_copy(wproj_hbm.at[b], wproj, psem)


def project_and_attend(pieces, piece, last, wqkv, normed, packed, attended):
    width = 3 * D // pieces

    @pl.loop(0, pieces)
    def _(n):
        for part in range(3 // pieces):
            piece(n * (3 // pieces) + part).wait()
        cols = pl.ds(pl.multiple_of(n * width, width), width)
        packed[:, cols] = jnp.dot(
            normed[...], wqkv[:, cols], preferred_element_type=F32
        ).astype(BF)

    @pl.loop(0, 2)
    def _(w):
        attend_windows(w * 8, 8, packed, attended)

    last.wait()


def local_kernel(
    b, x_hbm, gain_hbm, shift_hbm, wqkv_hbm, wproj_hbm, bias_hbm, out_ref, edge_ref,
    x_ref, gain, shift, bias, xsems, vsems, wqkv, wproj, normed, packed, attended, sems, psem,
):
    piece, last = weight_copies(b, wqkv_hbm, wproj_hbm, wqkv, wproj, sems, psem)
    vectors = [
        pltpu.make_async_copy(source, target, vsems.at[n])
        for n, (source, target) in enumerate(
            [(gain_hbm, gain), (shift_hbm, shift), (bias_hbm, bias)]
        )
    ]

    def tile(t):
        high = pl.ds(t // 4 * 8, 8)
        wide = pl.ds(pl.multiple_of(t % 4 * 16, 16), 16)
        return pltpu.make_async_copy(x_hbm.at[high, wide], x_ref.at[high, wide], xsems.at[t])

    tile(0).start()
    for copy in vectors:
        copy.start()
    for t in range(1, 8):
        tile(t).start()
    for copy in vectors:
        copy.wait()

    def norm(t):
        tile(t).wait()
        x = x_ref[pl.ds(t // 4 * 8, 8), pl.ds(pl.multiple_of(t % 4 * 16, 16), 16), :]
        x = x.astype(F32).reshape(8, 2, 8, D)
        for s in range(2):
            normed[pl.ds(pl.multiple_of(t * 128 + s * 64, 64), 64), :] = normalise(
                x[:, s].reshape(64, D), gain[b : b + 1], shift[b : b + 1]
            )

    pl.loop(0, 2, unroll=2)(norm)
    piece(0).start()
    pl.loop(2, 6, unroll=4)(norm)
    for n in range(1, 3 * D // NC):
        piece(n).start()
    last.start()
    pl.loop(6, 8, unroll=2)(norm)

    project_and_attend(3, piece, last, wqkv, normed, packed, attended)

    @pl.loop(0, D // NC)
    def _(n):
        cols = pl.ds(pl.multiple_of(n * NC, NC), NC)
        update = jnp.dot(attended[...], wproj[:, cols], preferred_element_type=F32)
        update = update + bias[b : b + 1, cols]
        for t in range(8):
            high, wide = slice(t // 4 * 8, t // 4 * 8 + 8), slice(t % 4 * 16, t % 4 * 16 + 16)
            x = x_ref[high, wide, cols].astype(F32).reshape(8, 2, 8, NC)
            for s in range(2):
                for r in range(8):
                    at = t * 128 + s * 64 + r * 8
                    tile = update[at : at + 8] + x[r, s]
                    for c in range(CHUNKS):
                        start = (t % 4 * 16 + s * 8) * PITCH + (t // 4 * 8 + r) * CHUNKS + c
                        part = tile[:, c * LANES : (c + 1) * LANES]
                        out_ref[pl.ds(start, 8, stride=PITCH), :] = part

    for side in range(2):
        start = (COLS - 2 + side) * PITCH
        column = out_ref[start : start + ROWS * CHUNKS, :]
        edge_ref[side * ROWS * CHUNKS : (side + 1) * ROWS * CHUNKS, :] = column.astype(BF)


ATTENTION_SCRATCH = [
    pltpu.VMEM((D, 3 * D), BF),
    pltpu.VMEM((D, D), BF),
    pltpu.VMEM((T, D), BF),
    pltpu.VMEM((T, 3 * D), BF),
    pltpu.VMEM((T, D), BF),
    pltpu.SemaphoreType.DMA((3 * D // NC,)),
    pltpu.SemaphoreType.DMA,
]


def local_attention(b, x, gain, shift, wqkv, wproj, bias):
    edge = jax.ShapeDtypeStruct((2 * ROWS * CHUNKS, LANES), BF)
    x, gain, shift, wqkv, wproj, bias = [
        pltpu.with_memory_space_constraint(a, pltpu.HBM)
        for a in (x, gain, shift, wqkv, wproj, bias)
    ]
    return pl.pallas_call(
        functools.partial(local_kernel, b),
        out_shape=(jax.ShapeDtypeStruct((COLS * PITCH, LANES), F32), edge),
        in_specs=[ANY] * 6,
        out_specs=(VM, VM),
        scratch_shapes=[
            pltpu.VMEM((ROWS, COLS, D), BF),
            pltpu.VMEM((2, D), F32),
            pltpu.VMEM((2, D), F32),
            pltpu.VMEM((2, D), F32),
            pltpu.SemaphoreType.DMA((8,)),
            pltpu.SemaphoreType.DMA((3,)),
        ]
        + ATTENTION_SCRATCH,
        compiler_params=pltpu.CompilerParams(vmem_limit_bytes=40 * 2**20),
        name="local_attention",
    )(x, gain, shift, wqkv, wproj, bias)


def place(col, row, chunk):
    return pl.ds(col * STRIDE + row * CHUNKS + chunk, 8, stride=STRIDE)


def widen(flat, wide):
    @pl.loop(0, 8)
    def _(n):
        rows = pl.ds(pl.multiple_of(n * 1152, 1152), 1152)
        wide[rows, :] = flat[rows, :].astype(F32)


def narrow(wide, flat):
    @pl.loop(0, 8)
    def _(n):
        rows = pl.ds(pl.multiple_of(n * 1152, 1152), 1152)
        flat[rows, :] = wide[rows, :].astype(BF)


def shuffled_kernel(
    b, in_ref, gain, shift, wqkv_hbm, wproj_hbm, bias, out_ref,
    wide, stream, wqkv, wproj, normed, packed, attended, sems, psem,
):
    piece, last = weight_copies(b, wqkv_hbm, wproj_hbm, wqkv, wproj, sems, psem)
    for n in range(3 * D // NC):
        piece(n).start()
    last.start()
    widen(in_ref, wide)

    @pl.loop(0, CHUNKS)
    def _(c):
        for i in range(7):
            above, below = i * 8, (i + 1) * 8
            wide[place(below, 1, c), :] += wide[place(above, EXT - 1, c), :]
            wide[place(above, EXT - 2, c), :] += wide[place(below, 0, c), :]

    @pl.loop(0, 16, unroll=8)
    def _(p):
        x = jnp.concatenate(
            [
                jnp.concatenate([wide[place(i * 8, p + 1, c), :] for c in range(CHUNKS)], axis=1)
                for i in range(8)
            ],
            axis=0,
        ).astype(BF)
        rows = pl.ds(pl.multiple_of(p * 64, 64), 64)
        stream[rows, :] = x
        normed[rows, :] = normalise(x.astype(F32), gain[b : b + 1], shift[b : b + 1])

    project_and_attend(1, piece, last, wqkv, normed, packed, attended)

    @pl.loop(0, D // NC)
    def _(n):
        cols = pl.ds(pl.multiple_of(n * NC, NC), NC)
        update = jnp.dot(attended[...], wproj[:, cols], preferred_element_type=F32)
        update = update + bias[b : b + 1, cols] + stream[:, cols].astype(F32)
        for u in range(NC // LANES):
            c = n * (NC // LANES) + u
            wide[place(0, 0, c), :] = jnp.zeros((8, LANES), F32)
            wide[place(56, EXT - 1, c), :] = jnp.zeros((8, LANES), F32)
            for p in range(16):
                for i in range(8):
                    tile = update[p * 64 + i * 8 : p * 64 + i * 8 + 8, u * LANES : (u + 1) * LANES]
                    wide[place(i * 8, p + 1, c), :] = tile
                    if p == 15 and i < 7:
                        wide[place(i * 8 + 8, 0, c), :] = tile
                    if p == 0 and i > 0:
                        wide[place(i * 8 - 8, EXT - 1, c), :] = tile

    narrow(wide, out_ref)


def shuffled_attention(b, x, gain, shift, wqkv, wproj, bias):
    return pl.pallas_call(
        functools.partial(shuffled_kernel, b),
        out_shape=jax.ShapeDtypeStruct((COLS * STRIDE, LANES), BF),
        in_specs=[VM, VM, VM, ANY, ANY, VM],
        out_specs=VM,
        scratch_shapes=[pltpu.VMEM((COLS * STRIDE, LANES), F32), pltpu.VMEM((T, D), BF)]
        + ATTENTION_SCRATCH,
        compiler_params=pltpu.CompilerParams(vmem_limit_bytes=48 * 2**20),
        name="shuffled_attention",
    )(
        x,
        gain,
        shift,
        pltpu.with_memory_space_constraint(wqkv, pltpu.HBM),
        pltpu.with_memory_space_constraint(wproj, pltpu.HBM),
        bias,
    )


def stage_taps(taps_ref, bias_ref, b, tiles):
    for c in range(CHUNKS):
        lanes = slice(c * LANES, (c + 1) * LANES)
        for t in range(9):
            tap = taps_ref[b, t : t + 1, lanes]
            tiles[t * 8 + c : t * 8 + c + 1, :] = tap + 1.0 if t == 4 else tap
        tiles[72 + c : 73 + c, :] = bias_ref[b : b + 1, lanes]


def column_sums(load, rows, low, high, taps):
    loaded = {}
    sums = []
    for row in rows:
        total = None
        for step in range(3):
            source = row + step - 1
            if low <= source < high:
                for col in range(3):
                    if (source, col) not in loaded:
                        loaded[source, col] = load(source, col)
                    term = taps[3 * step + col] * loaded[source, col]
                    total = term if total is None else total + term
        sums.append(total)
    return sums


def position():
    return lax.axis_index("pairs") * 2 + lax.axis_index("core")


def spread_column(k, load, tiles, out_ref, scales=(None, None, None)):
    taps = []
    for t in range(9):
        tap = tiles[t * 8 : t * 8 + 8, :]
        taps.append(tap if scales[t % 3] is None else tap * scales[t % 3])
    bias = tiles[72:80, :]
    sums = column_sums(load, range(-1, ROWS + 1), 0, ROWS, taps)
    sums[1:-1] = [total + bias for total in sums[1:-1]]
    for pair in range(EXT // 2):
        rows = pl.ds(pl.multiple_of(k * STRIDE + pair * 16, 16), 16)
        both = jnp.concatenate(sums[2 * pair : 2 * pair + 2], axis=0)
        out_ref[rows, :] = both.astype(BF)


def inner_spread_kernel(b, x_ref, taps_ref, bias_ref, out_ref, tiles):
    stage_taps(taps_ref, bias_ref, b, tiles)

    @pl.loop(2, COLS, unroll=2)
    def _(k):
        def load(r, col):
            return x_ref[pl.ds(pl.multiple_of((k + col - 2) * PITCH + r * 8, 8), 8), :]

        spread_column(k, load, tiles, out_ref)


def outer_spread_kernel(
    b, x_ref, edge_ref, taps_ref, bias_ref, _, out_ref, edge, held, tiles, sem
):
    inner = jnp.where(position() == 0, 0.0, 1.0)
    stage_taps(taps_ref, bias_ref, b, tiles)
    edge[...] = edge_ref[...].astype(F32)
    for k, scales in enumerate([(None, None, inner), (inner, None, None)]):

        def load(r, col):
            if k + col < 2:
                start = ((k + col) * ROWS + r) * CHUNKS
                return edge[start : start + 8, :]
            start = (k + col - 2) * PITCH + r * 8
            return x_ref[start : start + 8, :]

        spread_column(k, load, tiles, held, scales)
    copy = pltpu.make_async_copy(held, out_ref.at[pl.ds(0, 2 * STRIDE)], sem)
    copy.start()
    copy.wait()


def spread_convolution(b, x, edge, taps, bias):
    out = jax.ShapeDtypeStruct((COLS * STRIDE, LANES), BF)
    params = pltpu.CompilerParams(vmem_limit_bytes=24 * 2**20)
    inner = pl.pallas_call(
        functools.partial(inner_spread_kernel, b),
        out_shape=out,
        in_specs=[VM] * 3,
        out_specs=VM,
        scratch_shapes=[pltpu.VMEM((80, LANES), F32)],
        compiler_params=params,
        cost_estimate=pl.CostEstimate(flops=10**9, bytes_accessed=10**7, transcendentals=0),
        name="inner_spread_convolution",
    )(x, taps, bias)
    return pl.pallas_call(
        functools.partial(outer_spread_kernel, b),
        out_shape=out,
        in_specs=[VM] * 4 + [ANY],
        out_specs=ANY,
        scratch_shapes=[
            pltpu.VMEM((2 * ROWS * CHUNKS, LANES), F32),
            pltpu.VMEM((2 * STRIDE, LANES), BF),
            pltpu.VMEM((80, LANES), F32),
            pltpu.SemaphoreType.DMA,
        ],
        input_output_aliases={4: 0},
        compiler_params=params,
        name="outer_spread_convolution",
    )(x, edge, taps, bias, inner)


FIRST = 48


def columns_out(source, out_ref, first, sem):
    return pltpu.make_async_copy(source, out_ref.at[:, pl.ds(first, 16)], sem)


def final_columns(n, b, wide, natural, tiles, target):
    @pl.loop(0, 16, unroll=4)
    def _(w):
        taps = [tiles[t * 8 : t * 8 + 8, :] for t in range(9)]
        bias = tiles[72:80, :]

        def load(r, col):
            start = (n * 16 + w + col) * STRIDE + r * 8
            return wide[pl.ds(pl.multiple_of(start, 8), 8), :]

        sums = column_sums(load, range(1, EXT - 1), 0, EXT, taps)
        for row in range(ROWS):
            start = row * 128 + w // 8 * 64 + w % 8
            natural[pl.ds(start, 8, stride=8), :] = sums[row] + bias

    for row in range(ROWS):
        for c in range(CHUNKS):
            start = row * 128 + c * 8
            both = jnp.concatenate(
                [natural[start : start + 8, :], natural[start + 64 : start + 72, :]], axis=0
            )
            target[row, :, c * LANES : (c + 1) * LANES] = both.astype(BF)


def first_final_kernel(
    b, in_ref, taps_ref, bias_ref, out_ref, tail_ref, wide, natural, held, tiles, sems
):
    inner = jnp.where(position() == 0, 0.0, 1.0)
    stage_taps(taps_ref, bias_ref, b, tiles)

    @pl.loop(0, (FIRST + 2) // 2)
    def _(n):
        rows = pl.ds(pl.multiple_of(n * 2 * STRIDE, 2 * STRIDE), 2 * STRIDE)
        wide[rows, :] = in_ref[rows, :].astype(F32)

    wide[:STRIDE, :] = wide[:STRIDE, :] * inner
    count = FIRST // 16 - 1
    copies = [columns_out(held.at[n], out_ref, n * 16, sems.at[n]) for n in range(count)]
    for n in range(count):
        final_columns(n, b, wide, natural, tiles, held.at[n])
        copies[n].start()
    final_columns(count, b, wide, natural, tiles, tail_ref)
    for copy in copies:
        copy.wait()


def second_final_kernel(
    b, in_ref, edge_ref, taps_ref, bias_ref, tail_ref, _, out_ref,
    wide, natural, held, tiles, sems,
):
    outer = jnp.where(position() == 15, 0.0, 1.0)
    tail = columns_out(tail_ref, out_ref, FIRST - 16, sems.at[0])
    tail.start()
    stage_taps(taps_ref, bias_ref, b, tiles)
    count = (COLS - FIRST) * STRIDE
    wide[:count, :] = in_ref[FIRST * STRIDE :, :].astype(F32)
    wide[count : count + STRIDE, :] = edge_ref[:STRIDE, :].astype(F32)
    wide[count + STRIDE :, :] = edge_ref[STRIDE:, :].astype(F32) * outer
    final_columns(0, b, wide, natural, tiles, held)
    own = columns_out(held, out_ref, FIRST, sems.at[1])
    own.start()
    tail.wait()
    own.wait()


def final_convolution(b, x, edge, taps, bias):
    out = jax.ShapeDtypeStruct((ROWS, COLS, D), BF)
    block = (ROWS, 16, D)
    params = pltpu.CompilerParams(vmem_limit_bytes=24 * 2**20)
    first, tail = pl.pallas_call(
        functools.partial(first_final_kernel, b),
        out_shape=(out, jax.ShapeDtypeStruct(block, BF)),
        in_specs=[VM] * 3,
        out_specs=(ANY, VM),
        scratch_shapes=[
            pltpu.VMEM(((FIRST + 2) * STRIDE, LANES), F32),
            pltpu.VMEM((ROWS * 128, LANES), F32),
            pltpu.VMEM((FIRST // 16 - 1,) + block, BF),
            pltpu.VMEM((80, LANES), F32),
            pltpu.SemaphoreType.DMA((FIRST // 16 - 1,)),
        ],
        compiler_params=params,
        cost_estimate=pl.CostEstimate(flops=10**9, bytes_accessed=10**7, transcendentals=0),
        name="first_final_convolution",
    )(x, taps, bias)
    return pl.pallas_call(
        functools.partial(second_final_kernel, b),
        out_shape=out,
        in_specs=[VM] * 5 + [ANY],
        out_specs=ANY,
        scratch_shapes=[
            pltpu.VMEM(((COLS - FIRST + 2) * STRIDE, LANES), F32),
            pltpu.VMEM((ROWS * 128, LANES), F32),
            pltpu.VMEM(block, BF),
            pltpu.VMEM((80, LANES), F32),
            pltpu.SemaphoreType.DMA((2,)),
        ],
        input_output_aliases={5: 0},
        compiler_params=params,
        name="second_final_convolution",
    )(x, edge, taps, bias, tail, first)


def shifted(columns, step):
    axes = ("pairs", "core")
    count = lax.axis_size(axes)
    return lax.ppermute(columns, axes, [(i, (i + step) % count) for i in range(count)])


def exchange(flat):
    blocks = flat.reshape(COLS, STRIDE, LANES)
    return lax.all_to_all(blocks, ("rows", "pairs"), split_axis=0, concat_axis=0, tiled=True)


def body(patches, gain, shift, wqkv, wproj, bias, taps, conv_bias):
    block_one, edge = local_attention(0, patches, gain, shift, wqkv, wproj, bias)
    outgoing = spread_convolution(0, block_one, shifted(edge, 1), taps, conv_bias)
    arrived = exchange(outgoing).reshape(COLS * STRIDE, LANES)
    returning = shuffled_attention(1, arrived, gain, shift, wqkv, wproj, bias)
    restored = exchange(returning).reshape(COLS * STRIDE, LANES)
    edge = shifted(restored[: 2 * STRIDE], -1)
    return final_convolution(1, restored, edge, taps, conv_bias)


def solution(mesh):
    grid = Mesh(mesh.devices.reshape(8, 8, 2), ("rows", "pairs", "core"))
    split = P("rows", ("pairs", "core"), None)
    return jax.shard_map(
        body,
        mesh=grid,
        in_specs=(split, P(), P(), P(), P(), P(), P(), P()),
        out_specs=split,
        check_vma=False,
    )
```
